32 devices in a mesh: gx: 16 (over z, x, core), gy: 2 (over y).
Axes of the slice: x: 2, y: 2, z: 4, core: 2. Of those that a mesh axis runs over, the one named last changes fastest.
Arguments:
- offsets: float32 [3, 16, 16, 512], P(None, 'gx', 'gy'), may hold values from 0 to 1
- masses: float32 [16, 16, 512], P('gx', 'gy'), may hold values from 0.02 to 0.2
- kernel: bfloat16 [36, 2, 36, 16, 1024], P(None, None, None, 'gx', 'gy'), may hold values from -1.2 to 3.2, as said below
Outputs:
- acceleration: float32 [3, 16, 16, 512], P(None, 'gx', 'gy')
The draws below stay inside these ranges and needn't reach their ends.
Inputs may be any that keep to these rules, and one draw needn't show every extreme that they name: `kernel`: G is Hermitian in the wavevector: the entry at -k (each component modulo the grid) is the complex conjugate of the entry at k; all entries at the zero wavevector are zero.
All inputs are finite; a program needn't handle non-finite values.
Results may differ from the reference program's by a relative error of at most 0.0003.
Values sent between devices are 32-bit elements; how exact they have to be, the bound alone decides.
A program may use at most 128 MiB of HBM per device.

```python
import math
import jax
import jax.numpy as jnp
from jax import lax

NX = 16
NY = 16
NZ = 64
BODIES = 8
MOMENTS = 36


KERNEL_GAIN = 0.5


def mirror_axes(values):
    for axis_index in (1, 2, 3):
        values = jnp.roll(jnp.flip(values, axis_index), 1, axis_index)
    return values


def draw_kernel(key, part):
    full_shape = (2, MOMENTS, NY, NZ, NX)
    channel = jnp.arange(MOMENTS, dtype=jnp.int32)
    anchor = (jnp.arange(NY)[:, None, None] == 0) & (jnp.arange(NZ)[None, :, None] == 0) & (jnp.arange(NX)[None, None, :] == 0)

    def one_row(row_index):
        row_key = jax.random.fold_in(key, row_index)
        noise_key, diagonal_key = jax.random.split(row_key)
        jitter = jnp.clip(0.4 * jax.random.normal(noise_key, full_shape, jnp.float32), -2.4, 2.4)
        diagonal = jnp.exp(jax.random.uniform(diagonal_key, (NY, NZ, NX), jnp.float32, 0.0, math.log(4.0)))
        real_part = jitter[0] + jnp.where((channel == row_index)[:, None, None, None], diagonal[None], 0.0)
        imag_part = jitter[1]
        real_part = 0.5 * (real_part + mirror_axes(real_part))
        imag_part = 0.5 * (imag_part - mirror_axes(imag_part))
        both_parts = jnp.stack([real_part, imag_part]) * KERNEL_GAIN
        both_parts = jnp.where(anchor[None, None], 0.0, both_parts)
        return both_parts.reshape(2, MOMENTS, NY, NZ * NX)
    return lax.map(one_row, jnp.arange(MOMENTS, dtype=jnp.int32)).astype(jnp.bfloat16)


def level_of(stream_key, extent, pieces, least, largest):
    gain = 1.0
    for dim, parts in pieces:
        draws = jax.random.uniform(jax.random.fold_in(jax.random.fold_in(stream_key, 6), dim), (parts,), jnp.float32, least / len(pieces), largest / len(pieces))
        gain = gain * jnp.repeat(jnp.exp(draws), extent[dim] // parts).reshape((-1,) + (1,) * (len(extent) - 1 - dim))
    return gain


def setup_inputs(seed: int = 0) -> dict:
    seeds = jax.random.split(jax.random.key(seed), 4)
    offsets = jnp.clip(1.0 * jax.random.uniform(seeds[0], (3, NX, NY, BODIES * NZ), jnp.float32) ** level_of(seeds[0], (3, NX, NY, BODIES * NZ), ((1, 16), (2, 2)), -0.2, 0.2), 0.0, 1.0)
    masses = jnp.clip(jnp.exp(math.log(0.2) - 2.3025851 * jax.random.uniform(seeds[1], (NX, NY, BODIES * NZ), jnp.float32) ** level_of(seeds[1], (NX, NY, BODIES * NZ), ((0, 16), (1, 2)), -0.2, 0.2)), 0.02, 0.2)
    kernel = draw_kernel(jax.random.fold_in(seeds[3], 71), 0)
    return dict(offsets=offsets, masses=masses, kernel=kernel)


SOFTEN = 0.5

def channel_list():
    listed = []
    for pow_z in range(2):
        for pow_x in range(6 - pow_z):
            for pow_y in range(6 - pow_z - pow_x):
                listed.append((pow_x, pow_y, pow_z))
    return listed

def powers(values, highest):
    result = [jnp.ones_like(values)]
    for degree in range(highest):
        result.append(result[-1] * values)
    return result

def far_accel(local_field, along_x, along_y, along_z):
    accel = [jnp.zeros_like(along_x[1]) for axis_index in range(3)]
    for chan_index, (pow_x, pow_y, pow_z) in enumerate(channel_list()):
        coefficient = local_field[chan_index][:, :, None, :]
        if pow_x > 0:
            accel[0] = accel[0] - coefficient * (pow_x * along_x[pow_x - 1] * along_y[pow_y] * along_z[pow_z])
        if pow_y > 0:
            accel[1] = accel[1] - coefficient * (pow_y * along_x[pow_x] * along_y[pow_y - 1] * along_z[pow_z])
        if pow_z > 0:
            accel[2] = accel[2] - coefficient * (along_x[pow_x] * along_y[pow_y])
    return jnp.stack(accel)

def near_accel(body_pos, mass_cells):
    summed = jnp.zeros_like(body_pos)
    for shift_x in (-1, 0, 1):
        for shift_y in (-1, 0, 1):
            for shift_z in (-1, 0, 1):
                source = jnp.roll(body_pos, (-shift_x, -shift_y, -shift_z), axis=(1, 2, 4))
                source_mass = jnp.roll(mass_cells, (-shift_x, -shift_y, -shift_z), axis=(0, 1, 3))
                offset_vec = jnp.array([shift_x, shift_y, shift_z], jnp.float32).reshape(3, 1, 1, 1, 1)

                def add_slot(slot_index, running):
                    start = slot_index.astype(jnp.int32)
                    other = lax.dynamic_slice_in_dim(source, start, 1, 3)
                    other_mass = lax.dynamic_slice_in_dim(source_mass, start, 1, 2)
                    separation = other + offset_vec - body_pos
                    distance_sq = lax.optimization_barrier(jnp.sum(separation * separation, axis=0)) + SOFTEN * SOFTEN
                    inverse_r = lax.rsqrt(distance_sq)
                    return running + separation * (other_mass * inverse_r * inverse_r * inverse_r)
                summed = lax.fori_loop(0, BODIES, add_slot, summed)
    return summed

def reference(offsets, masses, kernel):
    body_pos = offsets.reshape(3, NX, NY, BODIES, NZ)
    mass_cells = masses.reshape(NX, NY, BODIES, NZ)
    scaled = 2.0 * body_pos - 1.0
    along_x = powers(scaled[0], 5)
    along_y = powers(scaled[1], 5)
    along_z = powers(scaled[2], 1)
    listed = channel_list()
    moments = jnp.stack([lax.optimization_barrier(jnp.sum(mass_cells * (along_x[pow_x] * along_y[pow_y] * along_z[pow_z]), axis=2)) for pow_x, pow_y, pow_z in listed])
    spectrum = jnp.fft.fftn(moments, axes=(1, 2, 3))
    spectrum = jnp.transpose(spectrum, (0, 2, 3, 1)).reshape(len(listed), NY, NZ * NX)
    spec_real = jnp.real(spectrum)
    spec_imag = jnp.imag(spectrum)

    def apply_row(kernel_row):
        gain_real = kernel_row[0].astype(jnp.float32)
        gain_imag = kernel_row[1].astype(jnp.float32)
        out_real = lax.optimization_barrier(jnp.sum(gain_real * spec_real - gain_imag * spec_imag, axis=0))
        out_imag = lax.optimization_barrier(jnp.sum(gain_real * spec_imag + gain_imag * spec_real, axis=0))
        return (out_real, out_imag)
    local_real, local_imag = lax.map(apply_row, kernel)
    local_spec = lax.complex(local_real, local_imag).reshape(len(listed), NY, NZ, NX)
    local_spec = jnp.transpose(local_spec, (0, 3, 1, 2))
    local_field = jnp.real(jnp.fft.ifftn(local_spec, axes=(1, 2, 3)))
    far_part = far_accel(local_field, along_x, along_y, along_z)
    near_part = near_accel(body_pos, mass_cells)
    return (far_part + near_part).reshape(3, NX, NY, BODIES * NZ)
```

```python
import functools
import math

import jax
import jax.numpy as jnp
import numpy as np
from jax import lax
from jax.experimental import pallas as pl
from jax.experimental.pallas import tpu as pltpu
from jax.sharding import PartitionSpec as P

BODIES = 8
SOFTEN = 0.5
LANES = 128
MESH = pl.DeviceIdType.MESH
HIGHEST = lax.Precision.HIGHEST


def channel_list():
    listed = []
    for pow_z in range(2):
        for pow_x in range(6 - pow_z):
            for pow_y in range(6 - pow_z - pow_x):
                listed.append((pow_x, pow_y, pow_z))
    return listed


CHANNELS = channel_list()
COUNT = len(CHANNELS)
HALF = COUNT // 2


class Sizes:
    def __init__(self, n_gx, n_gy, planes_x, rows_y, row_width, waves):
        self.n_gx, self.n_gy = n_gx, n_gy
        self.rows_y = rows_y
        self.cells_z = row_width // BODIES
        self.width = row_width
        self.total_x = planes_x * n_gx
        self.total_y = rows_y * n_gy
        self.kzw = self.cells_z // n_gy
        self.q = LANES // (2 * self.kzw)
        self.groups = waves // LANES
        self.wg = LANES // self.total_x
        self.rows = -(-COUNT // self.q)
        self.rows_pad = -(-self.rows // 8) * 8
        self.prow = -(-HALF // self.q)
        self.prow_pad = -(-self.prow // 8) * 8
        assert planes_x == 1 and self.total_y == n_gx and rows_y == 8
        assert 2 * self.cells_z == LANES and self.q % 2 == 0
        assert 2 * self.q * self.groups == self.total_x


def angle(left, right, length):
    return (np.multiply.outer(left, right) % length) * (2.0 * math.pi / length)


def tables(z):
    cells, kzw, q, wg, nx = z.cells_z, z.kzw, z.q, z.wg, z.total_x
    zf = np.zeros((z.n_gy, q // 2, 2, cells, 2, q, kzw))
    for h in range(z.n_gy):
        ang = angle(np.arange(cells), h * kzw + np.arange(kzw), cells)
        for u in range(q // 2):
            for b in range(2):
                zf[h, u, b, :, 0, 2 * u + b] = np.cos(ang)
                zf[h, u, b, :, 1, 2 * u + b] = -np.sin(ang)
    zf = zf.reshape(z.n_gy, q // 2, LANES, LANES)
    ang = angle(np.arange(nx), np.arange(nx), nx)
    c, s = np.cos(ang), np.sin(ang)
    xf = np.zeros((2, nx, wg, 2, wg, nx))
    xi = np.zeros((2, wg, nx, 2, nx, wg))
    for k in range(wg):
        xf[0, :, k, 0, k], xf[1, :, k, 0, k] = c, s
        xf[0, :, k, 1, k], xf[1, :, k, 1, k] = -s, c
        xi[0, k, :, 0, :, k], xi[1, k, :, 0, :, k] = c, -s
        xi[0, k, :, 1, :, k], xi[1, k, :, 1, :, k] = s, c
    xf = xf.reshape(2 * LANES, 2 * LANES)
    xi = xi.reshape(2 * LANES, 2 * LANES)
    zi = np.zeros((z.n_gy, 2, q, kzw, q, 2, 2, cells))
    scale = 1.0 / (z.total_x * z.total_y * cells)
    for h in range(z.n_gy):
        ang = angle(h * kzw + np.arange(kzw), np.arange(cells), cells)
        c, s = np.cos(ang) * scale, np.sin(ang) * scale
        for i in range(q):
            for copy in range(2):
                zi[h, 0, i, :, i, 0, copy], zi[h, 1, i, :, i, 0, copy] = c, -s
                zi[h, 0, i, :, i, 1, copy], zi[h, 1, i, :, i, 1, copy] = s, c
    zi = zi.reshape(z.n_gy, LANES, q * 2 * LANES)
    return [np.asarray(t, np.float32) for t in (zf, xf, xi, zi)]


def dot(left, right):
    return jnp.dot(left, right, precision=HIGHEST, preferred_element_type=jnp.float32)


def times_i(value, sign):
    return pltpu.roll(value, LANES // 2, 1) * sign


def transform(values, direction, sign):
    count = len(values)
    if count == 1:
        return values
    even = transform(values[0::2], direction, sign)
    odd = transform(values[1::2], direction, sign)
    low, high = [], []
    for k in range(count // 2):
        value = odd[k]
        if k * 4 == count:
            value = times_i(value, sign * direction)
        elif k:
            theta = direction * 2.0 * math.pi * k / count
            value = value * math.cos(theta) + times_i(value, sign * math.sin(theta))
        low.append(even[k] + value)
        high.append(even[k] - value)
    return low + high


def exchange(values, lane, chunk):
    count = len(values)
    values = list(values)
    bit = 1
    while bit < count:
        keep = (lane // (chunk * bit)) % 2 == 0
        for i in range(count):
            if i & bit == 0:
                a, b = values[i], values[i | bit]
                values[i] = jnp.where(keep, a, pltpu.roll(b, chunk * bit, 1))
                values[i | bit] = jnp.where(keep, pltpu.roll(a, LANES - chunk * bit, 1), b)
        bit *= 2
    return values


def lane_tiles(value):
    return [value[:, i : i + LANES] for i in range(0, value.shape[1], LANES)]


def powers(value, highest):
    result = [None, value]
    for _ in range(highest - 1):
        result.append(result[-1] * value)
    return result


def scaled_mul(value, power):
    return value if power is None else value * power


def kernel_body(
    z, off_hbm, mass_hbm, gain_hbm, zf_hbm, xf_hbm, xi_hbm, zi_hbm, out_ref,
    off_ref, mass_ref, gain, zf, xf, xi, zi, yb, edge, xh, xc, near_src, acc_ref, mom, msg_b, got_b, spec, coef,
    msg_c, got_c, lines, field,
    load_sem, ysend, yrecv, hsend, hrecv, csend, crecv, bsend, brecv, fsend, frecv,
):
    nx, ny = z.n_gx, z.n_gy
    mx, my = lax.axis_index("gx"), lax.axis_index("gy")
    me = mx * ny + my
    total = nx * ny

    def peer(k):
        other = lax.rem(me + k, total)
        return other // ny, lax.rem(other, ny)

    barrier = pltpu.get_barrier_semaphore()

    def greet(k, carry):
        px, py = peer(k)
        pl.semaphore_signal(barrier, inc=1, device_id=(px, py), device_id_type=MESH)
        return carry

    loads = [
        pltpu.make_async_copy(src, dst, load_sem.at[i])
        for i, (src, dst) in enumerate(
            [(off_hbm, off_ref), (mass_hbm, mass_ref), (zf_hbm.at[my], zf), (xf_hbm, xf), (xi_hbm, xi),
             (zi_hbm, zi), (gain_hbm, gain)]
        )
    ]
    for load in loads:
        load.start()
    lax.fori_loop(1, total, greet, 0)
    loads[0].wait()
    loads[1].wait()

    for comp in range(4):
        value = off_ref[comp] if comp < 3 else mass_ref[...]
        yb[my, comp] = value
        edge[0, comp] = value[0:1]
        edge[1, comp] = value[z.rows_y - 1 : z.rows_y]

    pl.semaphore_wait(barrier, total - 1)

    y_copies = []
    for k in range(1, ny):
        to = lax.rem(my + k, ny)
        copy = pltpu.make_async_remote_copy(
            src_ref=yb.at[my], dst_ref=yb.at[my], send_sem=ysend.at[k], recv_sem=yrecv.at[my],
            device_id=(mx, to), device_id_type=MESH,
        )
        copy.start()
        y_copies.append(copy)
    h_copies = []
    for side in range(2):
        to_x = lax.rem(mx + (1 if side == 0 else nx - 1), nx)
        copy = pltpu.make_async_remote_copy(
            src_ref=yb.at[my], dst_ref=xh.at[side], send_sem=hsend.at[side], recv_sem=hrecv.at[side],
            device_id=(to_x, my), device_id_type=MESH,
        )
        copy.start()
        h_copies.append(copy)
        for end in range(2):
            to_y = lax.rem(my + (1 if end == 0 else ny - 1), ny)
            copy = pltpu.make_async_remote_copy(
                src_ref=edge.at[1 - end], dst_ref=xc.at[side, end], send_sem=csend.at[side, end],
                recv_sem=crecv.at[side, end], device_id=(to_x, to_y), device_id_type=MESH,
            )
            copy.start()
            h_copies.append(copy)

    lane = lax.broadcasted_iota(jnp.int32, (1, LANES), 1)
    first = lane < LANES // 2
    sign = jnp.where(first, -1.0, 1.0).astype(jnp.float32)
    rows, rows_pad = z.rows, z.rows_pad

    if rows_pad != rows:
        mom[...] = jnp.zeros_like(mom)

    def moments_of(block, slot):
        bodies = [yb[block, comp] for comp in range(4)]
        s, t, w = [2.0 * v - 1.0 for v in bodies[:3]]
        along_x, along_y = powers(s, 5), powers(t, 5)
        made = {}
        weighted = bodies[3]
        for e in range(2):
            if e:
                weighted = weighted * w
            for a in range(6 - e):
                partial = scaled_mul(weighted, along_x[a] if a else None)
                for b in range(6 - e - a):
                    tiles = lane_tiles(scaled_mul(partial, along_y[b] if b else None))
                    made[(a, b, e)] = functools.reduce(lambda x, y: x + y, tiles)
        for u in range(z.q // 2):
            for r in range(rows):
                pair = []
                for b in range(2):
                    c = (2 * u + b) * rows + r
                    pair.append(made[CHANNELS[c]] if c < COUNT else jnp.zeros_like(s[:, :LANES]))
                mixed = jnp.where(first, pair[0], pair[1])
                crossed = jnp.where(first, pair[1], pair[0])
                mixed = mixed + pltpu.roll(crossed, LANES // 2, 1)
                mom[u, slot, pl.ds(r, z.rows_y, stride=rows_pad), :] = mixed

    moments_of(my, my)
    for k in range(1, ny):
        source = lax.rem(my + k, ny)
        pltpu.make_async_remote_copy(
            src_ref=yb.at[source], dst_ref=yb.at[source], send_sem=ysend.at[k], recv_sem=yrecv.at[source],
            device_id=(mx, source), device_id_type=MESH,
        ).wait_recv()
        moments_of(source, source)
    loads[2].wait()
    height = ny * z.rows_y * rows_pad
    along = dot(mom[0].reshape(height, LANES), zf[0])
    for u in range(1, z.q // 2):
        along = along + dot(mom[u].reshape(height, LANES), zf[u])
    along = [along[i * rows_pad : (i + 1) * rows_pad] for i in range(z.total_y)]
    for ky, value in enumerate(transform(along, -1.0, sign)):
        msg_b[ky] = value[:rows]

    def send_b(k, carry):
        to = lax.rem(mx + k, nx)
        pltpu.make_async_remote_copy(
            src_ref=msg_b.at[to], dst_ref=got_b.at[mx], send_sem=bsend.at[to], recv_sem=brecv.at[mx],
            device_id=(to, my), device_id_type=MESH,
        ).start()
        return carry

    lax.fori_loop(1, nx, send_b, 0)
    got_b[mx] = msg_b[mx]

    ahead, behind = lax.rem(my + 1, ny), lax.rem(my + ny - 1, ny)

    def fill(dx, main, top, bottom):
        for comp in range(4):
            value = main(comp)
            below = jnp.concatenate([top(comp), value[: z.rows_y - 1]], axis=0)
            above = jnp.concatenate([value[1:], bottom(comp)], axis=0)
            for dy, moved in enumerate((below, value, above)):
                if comp == 0 and dx != 1:
                    moved = moved + (dx - 1.0)
                if comp == 1 and dy != 1:
                    moved = moved + (dy - 1.0)
                for j, tile in enumerate(lane_tiles(moved)):
                    near_src[(dx * 3 + dy) * (z.width // LANES) + j, comp] = tile

    tiles = z.width // LANES

    def near_steps(begin, end):
        target = [[off_ref[comp, :, j * LANES : (j + 1) * LANES] for j in range(tiles)] for comp in range(3)]
        init = tuple(acc_ref[comp, :, j * LANES : (j + 1) * LANES] for comp in range(3) for j in range(tiles))

        def step(index, carry):
            sums = [list(carry[comp * tiles : (comp + 1) * tiles]) for comp in range(3)]
            loaded = [near_src[index, comp] for comp in range(4)]
            turned = [pltpu.roll(v, LANES // 2, 1) for v in loaded]
            for half in range(2):
                both = [
                    jnp.where(first, a, b) if half == 0 else jnp.where(first, b, a)
                    for a, b in zip(loaded, turned)
                ]
                for dz in (-1, 0, 1):
                    src = both if dz == 0 else [pltpu.roll(v, (LANES - dz) % LANES, 1) for v in both]
                    src_z = src[2] + float(dz) if dz else src[2]
                    for j in range(tiles):
                        sx = src[0] - target[0][j]
                        sy = src[1] - target[1][j]
                        sz = src_z - target[2][j]
                        inv = lax.rsqrt(sx * sx + sy * sy + (sz * sz + SOFTEN * SOFTEN))
                        pull = (src[3] * inv) * (inv * inv)
                        sums[0][j] = sums[0][j] + sx * pull
                        sums[1][j] = sums[1][j] + sy * pull
                        sums[2][j] = sums[2][j] + sz * pull
            return tuple(v for comp in sums for v in comp)

        final = lax.fori_loop(begin, end, step, init)
        for comp in range(3):
            for j in range(tiles):
                acc_ref[comp, :, j * LANES : (j + 1) * LANES] = final[comp * tiles + j]

    acc_ref[...] = jnp.zeros_like(acc_ref)
    fill(
        1,
        lambda comp: off_ref[comp] if comp < 3 else mass_ref[...],
        lambda comp: yb[behind, comp, z.rows_y - 1 : z.rows_y],
        lambda comp: yb[ahead, comp, 0:1],
    )
    near_steps(3 * tiles, 6 * tiles)
    for copy in h_copies:
        copy.wait_recv()
    for side in range(2):
        fill(2 * side, lambda comp: xh[side, comp], lambda comp: xc[side, 0, comp], lambda comp: xc[side, 1, comp])
    near_steps(0, 3 * tiles)

    def wait_b(k, carry):
        source = lax.rem(mx + k, nx)
        pltpu.make_async_remote_copy(
            src_ref=msg_b.at[source], dst_ref=got_b.at[source], send_sem=bsend.at[source],
            recv_sem=brecv.at[source], device_id=(source, my), device_id_type=MESH,
        ).wait_recv()
        return carry

    lax.fori_loop(1, nx, wait_b, 0)
    groups, q = z.groups, z.q
    turned = exchange([got_b[i] for i in range(nx)], lane, z.wg)
    loads[3].wait()
    stacked = jnp.concatenate(
        [
            jnp.concatenate([turned[(0 * q + i) * groups + g], turned[(1 * q + i) * groups + g]], axis=1)
            for g in range(groups)
            for i in range(q)
        ],
        axis=0,
    )
    spectrum = dot(stacked, xf[...])
    for g in range(groups):
        part = spectrum[g * q * rows : g * q * rows + COUNT]
        spec[0, g] = part[:, :LANES]
        spec[1, g] = part[:, LANES:]
    loads[6].wait()
    for g in range(groups):
        lanes = slice(g * LANES, (g + 1) * LANES)
        spec_re, spec_im = spec[0, g], spec[1, g]

        def couple(d, carry):
            gain_re = gain[d, 0, :, lanes].astype(jnp.float32)
            gain_im = gain[d, 1, :, lanes].astype(jnp.float32)
            coef[0, g, pl.ds(d, 1), :] = jnp.sum(gain_re * spec_re - gain_im * spec_im, axis=0, keepdims=True)
            coef[1, g, pl.ds(d, 1), :] = jnp.sum(gain_re * spec_im + gain_im * spec_re, axis=0, keepdims=True)
            return carry

        lax.fori_loop(0, COUNT, couple, 0, unroll=6)
    prow = z.prow
    height = q * prow
    pairs = []
    for g in range(groups):
        pair_re = coef[0, g, :HALF] - coef[1, g, HALF:]
        pair_im = coef[1, g, :HALF] + coef[0, g, HALF:]
        pair = jnp.concatenate([pair_re, pair_im], axis=1)
        if height > HALF:
            pair = jnp.concatenate([pair, jnp.zeros((height - HALF, 2 * LANES), jnp.float32)], axis=0)
        pairs.append(pair)
    loads[4].wait()
    back = dot(jnp.concatenate(pairs, axis=0), xi[...])
    ordered = [
        back[g * height + i * prow : g * height + (i + 1) * prow, ri * LANES : (ri + 1) * LANES]
        for ri in range(2)
        for i in range(q)
        for g in range(groups)
    ]
    for x, value in enumerate(exchange(ordered, lane, z.wg)):
        msg_c[x] = value

    def send_c(k, carry):
        px, py = peer(k)
        pltpu.make_async_remote_copy(
            src_ref=msg_c.at[px], dst_ref=got_c.at[my, mx], send_sem=fsend.at[py, px], recv_sem=frecv.at[my, mx],
            device_id=(px, py), device_id_type=MESH,
        ).start()
        return carry

    lax.fori_loop(1, total, send_c, 0)
    got_c[my, mx] = msg_c[mx]

    near_steps(6 * tiles, 9 * tiles)

    def wait_c(k, carry):
        px, py = peer(k)
        pltpu.make_async_remote_copy(
            src_ref=msg_c.at[px], dst_ref=got_c.at[py, px], send_sem=fsend.at[py, px], recv_sem=frecv.at[py, px],
            device_id=(px, py), device_id_type=MESH,
        ).wait_recv()
        return carry

    lax.fori_loop(1, total, wait_c, 0)
    loads[5].wait()
    prow_pad = z.prow_pad
    if prow_pad != prow:
        lines[:, :, prow:, :] = jnp.zeros(lines.shape[:2] + (prow_pad - prow, LANES), jnp.float32)
    result = None
    for h in range(ny):
        for y, value in enumerate(transform([got_c[h, k] for k in range(nx)], 1.0, sign)):
            lines[h, y, :prow] = value
        own = lines[h, pl.ds(my * z.rows_y, z.rows_y)].reshape(z.rows_y * prow_pad, LANES)
        term = dot(own, zi[h])
        result = term if result is None else result + term
    for column, tile in enumerate(lane_tiles(result)):
        field[column] = tile

    def coefficient(c):
        part, p = c // HALF, c % HALF
        i, r = p // prow, p % prow
        return field[i * 2 + part, pl.ds(r, z.rows_y, stride=prow_pad), :]

    number = {channel: c for c, channel in enumerate(CHANNELS)}
    for j in range(tiles):
        lanes = slice(j * LANES, (j + 1) * LANES)
        s, t, w = [2.0 * off_ref[comp, :, lanes] - 1.0 for comp in range(3)]
        along = []
        for e in range(2):
            value = slope_x = slope_y = None
            for b in reversed(range(6 - e)):
                top = 5 - e - b
                inner = coefficient(number[(top, b, e)])
                slope = None
                for a in reversed(range(top)):
                    slope = inner if slope is None else slope * s + inner
                    inner = inner * s + coefficient(number[(a, b, e)])
                slope_y = value if slope_y is None else slope_y * t + value
                value = inner if value is None else value * t + inner
                if slope is not None:
                    slope_x = slope if slope_x is None else slope_x * t + slope
            along.append((value, slope_x, slope_y))
        out_ref[0, :, lanes] = acc_ref[0, :, lanes] - (along[0][1] + w * along[1][1])
        out_ref[1, :, lanes] = acc_ref[1, :, lanes] - (along[0][2] + w * along[1][2])
        out_ref[2, :, lanes] = acc_ref[2, :, lanes] - along[1][0]

    for copy in y_copies:
        copy.wait_send()
    for copy in h_copies:
        copy.wait_send()

    def drain_b(k, carry):
        to = lax.rem(mx + k, nx)
        pltpu.make_async_remote_copy(
            src_ref=msg_b.at[to], dst_ref=got_b.at[mx], send_sem=bsend.at[to], recv_sem=brecv.at[mx],
            device_id=(to, my), device_id_type=MESH,
        ).wait_send()
        return carry

    lax.fori_loop(1, nx, drain_b, 0)

    def drain_c(k, carry):
        px, py = peer(k)
        pltpu.make_async_remote_copy(
            src_ref=msg_c.at[px], dst_ref=got_c.at[my, mx], send_sem=fsend.at[py, px], recv_sem=frecv.at[my, mx],
            device_id=(px, py), device_id_type=MESH,
        ).wait_send()
        return carry

    lax.fori_loop(1, total, drain_c, 0)


def local(offsets, masses, kernel):
    n_gx, n_gy = lax.axis_size("gx"), lax.axis_size("gy")
    _, planes_x, rows_y, width = offsets.shape
    waves = kernel.shape[3] * kernel.shape[4]
    z = Sizes(n_gx, n_gy, planes_x, rows_y, width, waves)
    made = tables(z)
    f32 = jnp.float32
    tiles = width // LANES
    scratch = [
        pltpu.VMEM((3, rows_y, width), f32),
        pltpu.VMEM((rows_y, width), f32),
        pltpu.VMEM((COUNT, 2, COUNT, waves), kernel.dtype),
        pltpu.VMEM(made[0].shape[1:], f32),
        pltpu.VMEM(made[1].shape, f32),
        pltpu.VMEM(made[2].shape, f32),
        pltpu.VMEM(made[3].shape, f32),
        pltpu.VMEM((n_gy, 4, rows_y, width), f32),
        pltpu.VMEM((2, 4, 1, width), f32),
        pltpu.VMEM((2, 4, rows_y, width), f32),
        pltpu.VMEM((2, 2, 4, 1, width), f32),
        pltpu.VMEM((9 * tiles, 4, rows_y, LANES), f32),
        pltpu.VMEM((3, rows_y, width), f32),
        pltpu.VMEM((z.q // 2, n_gy, rows_y * z.rows_pad, LANES), f32),
        pltpu.VMEM((n_gx, z.rows, LANES), f32),
        pltpu.VMEM((n_gx, z.rows, LANES), f32),
        pltpu.VMEM((2, z.groups, COUNT, LANES), f32),
        pltpu.VMEM((2, z.groups, COUNT, LANES), f32),
        pltpu.VMEM((n_gx, z.prow, LANES), f32),
        pltpu.VMEM((n_gy, n_gx, z.prow, LANES), f32),
        pltpu.VMEM((n_gy, n_gx, z.prow_pad, LANES), f32),
        pltpu.VMEM((z.q * 2, rows_y * z.prow_pad, LANES), f32),
        pltpu.SemaphoreType.DMA((7,)),
        pltpu.SemaphoreType.DMA((n_gy,)),
        pltpu.SemaphoreType.DMA((n_gy,)),
        pltpu.SemaphoreType.DMA((2,)),
        pltpu.SemaphoreType.DMA((2,)),
        pltpu.SemaphoreType.DMA((2, 2)),
        pltpu.SemaphoreType.DMA((2, 2)),
        pltpu.SemaphoreType.DMA((n_gx,)),
        pltpu.SemaphoreType.DMA((n_gx,)),
        pltpu.SemaphoreType.DMA((n_gy, n_gx)),
        pltpu.SemaphoreType.DMA((n_gy, n_gx)),
    ]
    out = pl.pallas_call(
        functools.partial(kernel_body, z),
        out_shape=jax.ShapeDtypeStruct((3, rows_y, width), f32),
        in_specs=[pl.BlockSpec(memory_space=pl.ANY)] * 7,
        out_specs=pl.BlockSpec(memory_space=pltpu.VMEM),
        scratch_shapes=scratch,
        compiler_params=pltpu.CompilerParams(
            collective_id=0, has_side_effects=True, vmem_limit_bytes=48 * 1024 * 1024
        ),
    )(
        offsets.reshape(3, rows_y, width), masses.reshape(rows_y, width),
        kernel.reshape(COUNT, 2, COUNT, waves), *[jnp.asarray(t) for t in made],
    )
    return out.reshape(3, planes_x, rows_y, width)


def solution(mesh):
    placed = (P(None, "gx", "gy", None), P("gx", "gy", None), P(None, None, None, "gx", "gy"))
    return jax.shard_map(
        local, mesh=mesh, in_specs=placed, out_specs=P(None, "gx", "gy", None), check_vma=False
    )
```

```python
import functools
import math

import jax
import jax.numpy as jnp
import numpy as np
from jax import lax
from jax.experimental import pallas as pl
from jax.experimental.pallas import tpu as pltpu
from jax.sharding import PartitionSpec as P

BODIES = 8
SOFTEN = 0.5
LANES = 128
PER_STEP = 2
MESH = pl.DeviceIdType.MESH


def channel_list():
    listed = []
    for pow_z in range(2):
        for pow_x in range(6 - pow_z):
            for pow_y in range(6 - pow_z - pow_x):
                listed.append((pow_x, pow_y, pow_z))
    return listed


CHANNELS = channel_list()
COUNT = len(CHANNELS)
HALF = COUNT // 2


class Sizes:
    def __init__(self, n_gx, n_gy, planes_x, rows_y, row_width, waves):
        self.n_gx, self.n_gy = n_gx, n_gy
        self.rows_y = rows_y
        self.cells_z = row_width // BODIES
        self.width = row_width
        self.total_x = planes_x * n_gx
        self.total_y = rows_y * n_gy
        self.kzw = self.cells_z // n_gy
        self.q = LANES // (2 * self.kzw)
        self.groups = waves // LANES
        self.wg = LANES // self.total_x
        self.rows = -(-COUNT // self.q)
        self.rows_pad = -(-self.rows // 8) * 8
        self.prow = -(-HALF // self.q)
        self.prow_pad = -(-self.prow // 8) * 8
        assert planes_x == 1 and self.total_y == n_gx and rows_y == 8
        assert 2 * self.cells_z == LANES and self.q % 2 == 0
        assert 2 * self.q * self.groups == self.total_x and self.groups == 4


def angle(left, right, length):
    return (np.multiply.outer(left, right) % length) * (2.0 * math.pi / length)


def two_terms(table, dim):
    table = np.asarray(table, np.float32)
    high = table.astype(jnp.bfloat16)
    low = (table - high.astype(np.float32)).astype(jnp.bfloat16)
    return np.concatenate([high, low], axis=dim)


def tables(z):
    cells, kzw, q, wg, nx = z.cells_z, z.kzw, z.q, z.wg, z.total_x
    zf = np.zeros((z.n_gy, q // 2, 2, cells, 2, q, kzw))
    for h in range(z.n_gy):
        ang = angle(np.arange(cells), h * kzw + np.arange(kzw), cells)
        for u in range(q // 2):
            for b in range(2):
                zf[h, u, b, :, 0, 2 * u + b] = np.cos(ang)
                zf[h, u, b, :, 1, 2 * u + b] = -np.sin(ang)
    zf = two_terms(zf.reshape(z.n_gy, q // 2, 1, LANES, LANES), 2)
    ang = angle(np.arange(nx), np.arange(nx), nx)
    c, s = np.cos(ang), np.sin(ang)
    xf = np.zeros((2, nx, wg, 2, wg, nx))
    xi = np.zeros((2, wg, nx, 2, nx, wg))
    for k in range(wg):
        xf[0, :, k, 0, k], xf[1, :, k, 0, k] = c, s
        xf[0, :, k, 1, k], xf[1, :, k, 1, k] = -s, c
        xi[0, k, :, 0, :, k], xi[1, k, :, 0, :, k] = c, -s
        xi[0, k, :, 1, :, k], xi[1, k, :, 1, :, k] = s, c
    xf = two_terms(xf.reshape(1, 2 * LANES, 2 * LANES), 0)
    xi = two_terms(xi.reshape(1, 2 * LANES, 2 * LANES), 0)
    zi = np.zeros((z.n_gy, 2, q, kzw, q, 2, 2, cells))
    scale = 1.0 / (z.total_x * z.total_y * cells)
    for h in range(z.n_gy):
        ang = angle(h * kzw + np.arange(kzw), np.arange(cells), cells)
        c, s = np.cos(ang) * scale, np.sin(ang) * scale
        for i in range(q):
            for copy in range(2):
                zi[h, 0, i, :, i, 0, copy], zi[h, 1, i, :, i, 0, copy] = c, -s
                zi[h, 0, i, :, i, 1, copy], zi[h, 1, i, :, i, 1, copy] = s, c
    zi = two_terms(zi.reshape(z.n_gy, 1, LANES, q * 2 * LANES), 1)
    return zf, xf, xi, zi


def split(value):
    high = value.astype(jnp.bfloat16)
    return high, (value - high.astype(jnp.float32)).astype(jnp.bfloat16)


def dot(left, right):
    high, low = split(left)

    def one(a, b):
        return jnp.dot(a, b, preferred_element_type=jnp.float32)

    return one(high, right[0]) + (one(high, right[1]) + one(low, right[0]))


def times_i(value, sign):
    return pltpu.roll(value, LANES // 2, 1) * sign


def transform(values, direction, sign):
    count = len(values)
    if count == 1:
        return values
    even = transform(values[0::2], direction, sign)
    odd = transform(values[1::2], direction, sign)
    low, high = [], []
    for k in range(count // 2):
        value = odd[k]
        if k * 4 == count:
            value = times_i(value, sign * direction)
        elif k:
            theta = direction * 2.0 * math.pi * k / count
            value = value * math.cos(theta) + times_i(value, sign * math.sin(theta))
        low.append(even[k] + value)
        high.append(even[k] - value)
    return low + high


def exchange(values, lane, chunk):
    count = len(values)
    values = list(values)
    bit = 1
    while bit < count:
        keep = (lane // (chunk * bit)) % 2 == 0
        for i in range(count):
            if i & bit == 0:
                a, b = values[i], values[i | bit]
                values[i] = jnp.where(keep, a, pltpu.roll(b, chunk * bit, 1))
                values[i | bit] = jnp.where(keep, pltpu.roll(a, LANES - chunk * bit, 1), b)
        bit *= 2
    return values


def lane_tiles(value):
    return [value[:, i : i + LANES] for i in range(0, value.shape[1], LANES)]


def powers(value, highest):
    result = [None, value]
    for _ in range(highest - 1):
        result.append(result[-1] * value)
    return result


def scaled_mul(value, power):
    return value if power is None else value * power


def kernel_body(
    z, off_hbm, mass_hbm, gain_hbm, zf_hbm, xf_hbm, xi_hbm, zi_hbm, out_ref,
    off_ref, mass_ref, gain, zf, xf, xi, zi, yb, edge, xh, xc, near_src, acc_ref, mom, msg_b, got_b, spec, coef,
    msg_c, got_c, lines, field,
    load_sem, ysend, yrecv, hsend, hrecv, csend, crecv, bsend, brecv, fsend, frecv,
):
    nx, ny = z.n_gx, z.n_gy
    mx, my = lax.axis_index("gx"), lax.axis_index("gy")
    me = mx * ny + my
    total = nx * ny

    def peer(k):
        other = lax.rem(me + k, total)
        return other // ny, lax.rem(other, ny)

    barrier = pltpu.get_barrier_semaphore()

    def greet(k, carry):
        px, py = peer(k)
        pl.semaphore_signal(barrier, inc=1, device_id=(px, py), device_id_type=MESH)
        return carry

    loads = [
        pltpu.make_async_copy(src, dst, load_sem.at[i])
        for i, (src, dst) in enumerate(
            [(off_hbm, off_ref), (mass_hbm, mass_ref), (zf_hbm.at[my], zf), (xf_hbm, xf), (xi_hbm, xi),
             (zi_hbm, zi), (gain_hbm, gain)]
        )
    ]
    for load in loads:
        load.start()
    lax.fori_loop(1, total, greet, 0)
    loads[0].wait()
    loads[1].wait()

    for comp in range(4):
        value = off_ref[comp] if comp < 3 else mass_ref[...]
        yb[my, comp] = value
        edge[0, comp] = value[0:1]
        edge[1, comp] = value[z.rows_y - 1 : z.rows_y]

    pl.semaphore_wait(barrier, total - 1)

    y_copies = []
    for k in range(1, ny):
        to = lax.rem(my + k, ny)
        copy = pltpu.make_async_remote_copy(
            src_ref=yb.at[my], dst_ref=yb.at[my], send_sem=ysend.at[k], recv_sem=yrecv.at[my],
            device_id=(mx, to), device_id_type=MESH,
        )
        copy.start()
        y_copies.append(copy)
    h_copies = []
    for side in range(2):
        to_x = lax.rem(mx + (1 if side == 0 else nx - 1), nx)
        copy = pltpu.make_async_remote_copy(
            src_ref=yb.at[my], dst_ref=xh.at[side], send_sem=hsend.at[side], recv_sem=hrecv.at[side],
            device_id=(to_x, my), device_id_type=MESH,
        )
        copy.start()
        h_copies.append(copy)
        for end in range(2):
            to_y = lax.rem(my + (1 if end == 0 else ny - 1), ny)
            copy = pltpu.make_async_remote_copy(
                src_ref=edge.at[1 - end], dst_ref=xc.at[side, end], send_sem=csend.at[side, end],
                recv_sem=crecv.at[side, end], device_id=(to_x, to_y), device_id_type=MESH,
            )
            copy.start()
            h_copies.append(copy)

    lane = lax.broadcasted_iota(jnp.int32, (1, LANES), 1)
    first = lane < LANES // 2
    sign = jnp.where(first, -1.0, 1.0).astype(jnp.float32)
    rows, rows_pad = z.rows, z.rows_pad

    if rows_pad != rows:
        mom[...] = jnp.zeros_like(mom)

    def moments_of(block, slot):
        bodies = [yb[block, comp] for comp in range(4)]
        s, t, w = [2.0 * v - 1.0 for v in bodies[:3]]
        along_x, along_y = powers(s, 5), powers(t, 5)
        made = {}
        weighted = bodies[3]
        for e in range(2):
            if e:
                weighted = weighted * w
            for a in range(6 - e):
                partial = scaled_mul(weighted, along_x[a] if a else None)
                for b in range(6 - e - a):
                    tiles = lane_tiles(scaled_mul(partial, along_y[b] if b else None))
                    made[(a, b, e)] = functools.reduce(lambda x, y: x + y, tiles)
        for u in range(z.q // 2):
            for r in range(rows):
                pair = []
                for b in range(2):
                    c = (2 * u + b) * rows + r
                    pair.append(made[CHANNELS[c]] if c < COUNT else jnp.zeros_like(s[:, :LANES]))
                mixed = jnp.where(first, pair[0], pair[1])
                crossed = jnp.where(first, pair[1], pair[0])
                mixed = mixed + pltpu.roll(crossed, LANES // 2, 1)
                mom[u, slot, pl.ds(r, z.rows_y, stride=rows_pad), :] = mixed

    moments_of(my, my)
    for k in range(1, ny):
        source = lax.rem(my + k, ny)
        pltpu.make_async_remote_copy(
            src_ref=yb.at[source], dst_ref=yb.at[source], send_sem=ysend.at[k], recv_sem=yrecv.at[source],
            device_id=(mx, source), device_id_type=MESH,
        ).wait_recv()
        moments_of(source, source)
    loads[2].wait()
    height = ny * z.rows_y * rows_pad
    along = dot(mom[0].reshape(height, LANES), zf.at[0])
    for u in range(1, z.q // 2):
        along = along + dot(mom[u].reshape(height, LANES), zf.at[u])
    along = [along[i * rows_pad : (i + 1) * rows_pad] for i in range(z.total_y)]
    for ky, value in enumerate(transform(along, -1.0, sign)):
        msg_b[ky] = value[:rows]

    def send_b(k, carry):
        to = lax.rem(mx + k, nx)
        pltpu.make_async_remote_copy(
            src_ref=msg_b.at[to], dst_ref=got_b.at[mx], send_sem=bsend.at[to], recv_sem=brecv.at[mx],
            device_id=(to, my), device_id_type=MESH,
        ).start()
        return carry

    lax.fori_loop(1, nx, send_b, 0)
    got_b[mx] = msg_b[mx]

    ahead, behind = lax.rem(my + 1, ny), lax.rem(my + ny - 1, ny)

    def fill(dx, main, top, bottom):
        for comp in range(4):
            value = main(comp)
            below = jnp.concatenate([top(comp), value[: z.rows_y - 1]], axis=0)
            above = jnp.concatenate([value[1:], bottom(comp)], axis=0)
            for dy, moved in enumerate((below, value, above)):
                if comp == 0 and dx != 1:
                    moved = moved + (dx - 1.0)
                if comp == 1 and dy != 1:
                    moved = moved + (dy - 1.0)
                for j, tile in enumerate(lane_tiles(moved)):
                    near_src[(dx * 3 + dy) * (z.width // LANES) + j, comp] = tile

    tiles = z.width // LANES

    def near_steps(begin, end):
        target = [[off_ref[comp, :, j * LANES : (j + 1) * LANES] for j in range(tiles)] for comp in range(3)]
        init = tuple(acc_ref[comp, :, j * LANES : (j + 1) * LANES] for comp in range(3) for j in range(tiles))

        def step(index, carry):
            sums = [list(carry[comp * tiles : (comp + 1) * tiles]) for comp in range(3)]
            loaded = [near_src[index, comp] for comp in range(4)]
            turned = [pltpu.roll(v, LANES // 2, 1) for v in loaded]
            for half in range(2):
                both = [
                    jnp.where(first, a, b) if half == 0 else jnp.where(first, b, a)
                    for a, b in zip(loaded, turned)
                ]
                for dz in (-1, 0, 1):
                    src = both if dz == 0 else [pltpu.roll(v, (LANES - dz) % LANES, 1) for v in both]
                    src_z = src[2] + float(dz) if dz else src[2]
                    for j in range(tiles):
                        sx = src[0] - target[0][j]
                        sy = src[1] - target[1][j]
                        sz = src_z - target[2][j]
                        inv = lax.rsqrt(sx * sx + sy * sy + (sz * sz + SOFTEN * SOFTEN))
                        pull = (src[3] * inv) * (inv * inv)
                        sums[0][j] = sums[0][j] + sx * pull
                        sums[1][j] = sums[1][j] + sy * pull
                        sums[2][j] = sums[2][j] + sz * pull
            return tuple(v for comp in sums for v in comp)

        final = lax.fori_loop(begin, end, step, init)
        for comp in range(3):
            for j in range(tiles):
                acc_ref[comp, :, j * LANES : (j + 1) * LANES] = final[comp * tiles + j]

    acc_ref[...] = jnp.zeros_like(acc_ref)
    fill(
        1,
        lambda comp: off_ref[comp] if comp < 3 else mass_ref[...],
        lambda comp: yb[behind, comp, z.rows_y - 1 : z.rows_y],
        lambda comp: yb[ahead, comp, 0:1],
    )
    near_steps(3 * tiles, 6 * tiles)
    for copy in h_copies:
        copy.wait_recv()
    for side in range(2):
        fill(2 * side, lambda comp: xh[side, comp], lambda comp: xc[side, 0, comp], lambda comp: xc[side, 1, comp])
    near_steps(0, 3 * tiles)

    def wait_b(k, carry):
        source = lax.rem(mx + k, nx)
        pltpu.make_async_remote_copy(
            src_ref=msg_b.at[source], dst_ref=got_b.at[source], send_sem=bsend.at[source],
            recv_sem=brecv.at[source], device_id=(source, my), device_id_type=MESH,
        ).wait_recv()
        return carry

    lax.fori_loop(1, nx, wait_b, 0)
    groups, q = z.groups, z.q
    deep = 2 * groups
    turned = exchange([got_b[i] for i in range(nx)], lane, z.wg)
    loads[3].wait()
    stacked = jnp.concatenate(
        [
            jnp.concatenate([turned[(0 * q + i) * groups + g], turned[(1 * q + i) * groups + g]], axis=1)
            for g in range(groups)
            for i in range(q)
        ],
        axis=0,
    )
    spectrum = dot(stacked, xf)
    for g in range(groups):
        part = spectrum[g * q * rows : g * q * rows + COUNT]
        part_re, part_im = part[:, :LANES], part[:, LANES:]
        for which, (front, back) in enumerate(((part_re, -part_im), (part_im, part_re))):
            spec[which, pl.ds(2 * g, COUNT, stride=deep), :] = front
            spec[which, pl.ds(2 * g + 1, COUNT, stride=deep), :] = back
    loads[6].wait()

    def couple(step, carry):
        members = [step * PER_STEP + i for i in range(PER_STEP)]
        sums = [[None, None] for _ in range(2 * PER_STEP)]
        for c in range(0, COUNT, 2):
            spec_two = [[spec[w, (c + i) * deep : (c + i + 1) * deep] for w in range(2)] for i in range(2)]
            for n in range(2 * PER_STEP):
                d = members[n // 2] + (n % 2) * HALF
                two = gain[d, c * deep : (c + 2) * deep, :].astype(jnp.float32)
                for i in range(2):
                    one = two[i * deep : (i + 1) * deep]
                    for w in range(2):
                        term = one * spec_two[i][w]
                        sums[n][w] = term if sums[n][w] is None else sums[n][w] + term
        for i, p in enumerate(members):
            own, other = sums[2 * i], sums[2 * i + 1]
            start = pl.multiple_of(p * deep, deep)
            coef[0, pl.ds(start, deep), :] = own[0] - other[1]
            coef[1, pl.ds(start, deep), :] = own[1] + other[0]
        return carry

    lax.fori_loop(0, HALF // PER_STEP, couple, 0)
    prow = z.prow
    height = q * prow
    pairs = []
    for g in range(groups):
        pair = jnp.concatenate(
            [
                coef[w, pl.ds(2 * g, HALF, stride=deep), :] + coef[w, pl.ds(2 * g + 1, HALF, stride=deep), :]
                for w in range(2)
            ],
            axis=1,
        )
        if height > HALF:
            pair = jnp.concatenate([pair, jnp.zeros((height - HALF, 2 * LANES), jnp.float32)], axis=0)
        pairs.append(pair)
    loads[4].wait()
    back = dot(jnp.concatenate(pairs, axis=0), xi)
    ordered = [
        back[g * height + i * prow : g * height + (i + 1) * prow, ri * LANES : (ri + 1) * LANES]
        for ri in range(2)
        for i in range(q)
        for g in range(groups)
    ]
    for x, value in enumerate(exchange(ordered, lane, z.wg)):
        msg_c[x] = value

    def send_c(k, carry):
        px, py = peer(k)
        pltpu.make_async_remote_copy(
            src_ref=msg_c.at[px], dst_ref=got_c.at[my, mx], send_sem=fsend.at[py, px], recv_sem=frecv.at[my, mx],
            device_id=(px, py), device_id_type=MESH,
        ).start()
        return carry

    lax.fori_loop(1, total, send_c, 0)
    got_c[my, mx] = msg_c[mx]

    near_steps(6 * tiles, 9 * tiles)

    def wait_c(k, carry):
        px, py = peer(k)
        pltpu.make_async_remote_copy(
            src_ref=msg_c.at[px], dst_ref=got_c.at[py, px], send_sem=fsend.at[py, px], recv_sem=frecv.at[py, px],
            device_id=(px, py), device_id_type=MESH,
        ).wait_recv()
        return carry

    lax.fori_loop(1, total, wait_c, 0)
    loads[5].wait()
    prow_pad = z.prow_pad
    if prow_pad != prow:
        lines[:, :, prow:, :] = jnp.zeros(lines.shape[:2] + (prow_pad - prow, LANES), jnp.float32)
    result = None
    for h in range(ny):
        for y, value in enumerate(transform([got_c[h, k] for k in range(nx)], 1.0, sign)):
            lines[h, y, :prow] = value
        own = lines[h, pl.ds(my * z.rows_y, z.rows_y)].reshape(z.rows_y * prow_pad, LANES)
        term = dot(own, zi.at[h])
        result = term if result is None else result + term
    for column, tile in enumerate(lane_tiles(result)):
        field[column] = tile

    def coefficient(c):
        part, p = c // HALF, c % HALF
        i, r = p // prow, p % prow
        return field[i * 2 + part, pl.ds(r, z.rows_y, stride=prow_pad), :]

    number = {channel: c for c, channel in enumerate(CHANNELS)}
    for j in range(tiles):
        lanes = slice(j * LANES, (j + 1) * LANES)
        s, t, w = [2.0 * off_ref[comp, :, lanes] - 1.0 for comp in range(3)]
        along = []
        for e in range(2):
            value = slope_x = slope_y = None
            for b in reversed(range(6 - e)):
                top = 5 - e - b
                inner = coefficient(number[(top, b, e)])
                slope = None
                for a in reversed(range(top)):
                    slope = inner if slope is None else slope * s + inner
                    inner = inner * s + coefficient(number[(a, b, e)])
                slope_y = value if slope_y is None else slope_y * t + value
                value = inner if value is None else value * t + inner
                if slope is not None:
                    slope_x = slope if slope_x is None else slope_x * t + slope
            along.append((value, slope_x, slope_y))
        out_ref[0, :, lanes] = acc_ref[0, :, lanes] - (along[0][1] + w * along[1][1])
        out_ref[1, :, lanes] = acc_ref[1, :, lanes] - (along[0][2] + w * along[1][2])
        out_ref[2, :, lanes] = acc_ref[2, :, lanes] - along[1][0]

    for copy in y_copies:
        copy.wait_send()
    for copy in h_copies:
        copy.wait_send()

    def drain_b(k, carry):
        to = lax.rem(mx + k, nx)
        pltpu.make_async_remote_copy(
            src_ref=msg_b.at[to], dst_ref=got_b.at[mx], send_sem=bsend.at[to], recv_sem=brecv.at[mx],
            device_id=(to, my), device_id_type=MESH,
        ).wait_send()
        return carry

    lax.fori_loop(1, nx, drain_b, 0)

    def drain_c(k, carry):
        px, py = peer(k)
        pltpu.make_async_remote_copy(
            src_ref=msg_c.at[px], dst_ref=got_c.at[my, mx], send_sem=fsend.at[py, px], recv_sem=frecv.at[my, mx],
            device_id=(px, py), device_id_type=MESH,
        ).wait_send()
        return carry

    lax.fori_loop(1, total, drain_c, 0)


def local(offsets, masses, kernel):
    n_gx, n_gy = lax.axis_size("gx"), lax.axis_size("gy")
    _, planes_x, rows_y, width = offsets.shape
    waves = kernel.shape[3] * kernel.shape[4]
    z = Sizes(n_gx, n_gy, planes_x, rows_y, width, waves)
    made = tables(z)
    f32, bf16 = jnp.float32, jnp.bfloat16
    tiles = width // LANES
    scratch = [
        pltpu.VMEM((3, rows_y, width), f32),
        pltpu.VMEM((rows_y, width), f32),
        pltpu.VMEM((COUNT, COUNT * 2 * z.groups, LANES), kernel.dtype),
        pltpu.VMEM(made[0].shape[1:], bf16),
        pltpu.VMEM(made[1].shape, bf16),
        pltpu.VMEM(made[2].shape, bf16),
        pltpu.VMEM(made[3].shape, bf16),
        pltpu.VMEM((n_gy, 4, rows_y, width), f32),
        pltpu.VMEM((2, 4, 1, width), f32),
        pltpu.VMEM((2, 4, rows_y, width), f32),
        pltpu.VMEM((2, 2, 4, 1, width), f32),
        pltpu.VMEM((9 * tiles, 4, rows_y, LANES), f32),
        pltpu.VMEM((3, rows_y, width), f32),
        pltpu.VMEM((z.q // 2, n_gy, rows_y * z.rows_pad, LANES), f32),
        pltpu.VMEM((n_gx, z.rows, LANES), f32),
        pltpu.VMEM((n_gx, z.rows, LANES), f32),
        pltpu.VMEM((2, COUNT * 2 * z.groups, LANES), f32),
        pltpu.VMEM((2, HALF * 2 * z.groups, LANES), f32),
        pltpu.VMEM((n_gx, z.prow, LANES), f32),
        pltpu.VMEM((n_gy, n_gx, z.prow, LANES), f32),
        pltpu.VMEM((n_gy, n_gx, z.prow_pad, LANES), f32),
        pltpu.VMEM((z.q * 2, rows_y * z.prow_pad, LANES), f32),
        pltpu.SemaphoreType.DMA((7,)),
        pltpu.SemaphoreType.DMA((n_gy,)),
        pltpu.SemaphoreType.DMA((n_gy,)),
        pltpu.SemaphoreType.DMA((2,)),
        pltpu.SemaphoreType.DMA((2,)),
        pltpu.SemaphoreType.DMA((2, 2)),
        pltpu.SemaphoreType.DMA((2, 2)),
        pltpu.SemaphoreType.DMA((n_gx,)),
        pltpu.SemaphoreType.DMA((n_gx,)),
        pltpu.SemaphoreType.DMA((n_gy, n_gx)),
        pltpu.SemaphoreType.DMA((n_gy, n_gx)),
    ]
    gains = jnp.transpose(kernel.reshape(COUNT, 2, COUNT, z.groups, LANES), (0, 2, 3, 1, 4))
    gains = gains.reshape(COUNT, COUNT * 2 * z.groups, LANES)
    out = pl.pallas_call(
        functools.partial(kernel_body, z),
        out_shape=jax.ShapeDtypeStruct((3, rows_y, width), f32),
        in_specs=[pl.BlockSpec(memory_space=pltpu.HBM)] * 7,
        out_specs=pl.BlockSpec(memory_space=pltpu.VMEM),
        scratch_shapes=scratch,
        compiler_params=pltpu.CompilerParams(
            collective_id=0, has_side_effects=True, vmem_limit_bytes=62 * 1024 * 1024
        ),
    )(
        offsets.reshape(3, rows_y, width), masses.reshape(rows_y, width),
        gains, *[jnp.asarray(t) for t in made],
    )
    return out.reshape(3, planes_x, rows_y, width)


def solution(mesh):
    placed = (P(None, "gx", "gy", None), P("gx", "gy", None), P(None, None, None, "gx", "gy"))
    return jax.shard_map(
        local, mesh=mesh, in_specs=placed, out_specs=P(None, "gx", "gy", None), check_vma=False
    )
```

```python
import functools
import math

import jax
import jax.numpy as jnp
import numpy as np
from jax import lax
from jax.experimental import pallas as pl
from jax.experimental.pallas import tpu as pltpu
from jax.sharding import PartitionSpec as P

BODIES = 8
SOFTEN = 0.5
LANES = 128
PER_STEP = 2
MESH = pl.DeviceIdType.MESH


def channel_list():
    listed = []
    for pow_z in range(2):
        for pow_x in range(6 - pow_z):
            for pow_y in range(6 - pow_z - pow_x):
                listed.append((pow_x, pow_y, pow_z))
    return listed


CHANNELS = channel_list()
COUNT = len(CHANNELS)
HALF = COUNT // 2


class Sizes:
    def __init__(self, n_gx, n_gy, planes_x, rows_y, row_width, waves):
        self.n_gx, self.n_gy = n_gx, n_gy
        self.rows_y = rows_y
        self.cells_z = row_width // BODIES
        self.width = row_width
        self.total_x = planes_x * n_gx
        self.total_y = rows_y * n_gy
        self.kzw = self.cells_z // n_gy
        self.q = LANES // (2 * self.kzw)
        self.groups = waves // LANES
        self.wg = LANES // self.total_x
        self.rows = -(-COUNT // self.q)
        self.rows_pad = -(-self.rows // 8) * 8
        self.prow = -(-HALF // self.q)
        self.prow_pad = -(-self.prow // 8) * 8
        assert planes_x == 1 and self.total_y == n_gx and rows_y == 8
        assert 2 * self.cells_z == LANES and self.q % 2 == 0
        assert 2 * self.q * self.groups == self.total_x and self.groups == 4


def angle(left, right, length):
    return (np.multiply.outer(left, right) % length) * (2.0 * math.pi / length)


def two_terms(table, dim):
    table = np.asarray(table, np.float32)
    high = table.astype(jnp.bfloat16)
    low = (table - high.astype(np.float32)).astype(jnp.bfloat16)
    return np.concatenate([high, low], axis=dim)


def tables(z):
    cells, kzw, q, wg, nx = z.cells_z, z.kzw, z.q, z.wg, z.total_x
    zf = np.zeros((z.n_gy, q // 2, 2, cells, 2, q, kzw))
    for h in range(z.n_gy):
        ang = angle(np.arange(cells), h * kzw + np.arange(kzw), cells)
        for u in range(q // 2):
            for b in range(2):
                zf[h, u, b, :, 0, 2 * u + b] = np.cos(ang)
                zf[h, u, b, :, 1, 2 * u + b] = -np.sin(ang)
    zf = two_terms(zf.reshape(z.n_gy, q // 2, 1, LANES, LANES), 2)
    ang = angle(np.arange(nx), np.arange(nx), nx)
    c, s = np.cos(ang), np.sin(ang)
    xf = np.zeros((2, nx, wg, 2, wg, nx))
    xi = np.zeros((2, wg, nx, 2, nx, wg))
    for k in range(wg):
        xf[0, :, k, 0, k], xf[1, :, k, 0, k] = c, s
        xf[0, :, k, 1, k], xf[1, :, k, 1, k] = -s, c
        xi[0, k, :, 0, :, k], xi[1, k, :, 0, :, k] = c, -s
        xi[0, k, :, 1, :, k], xi[1, k, :, 1, :, k] = s, c
    xf = two_terms(xf.reshape(1, 2 * LANES, 2 * LANES), 0)
    xi = two_terms(xi.reshape(1, 2 * LANES, 2 * LANES), 0)
    zi = np.zeros((z.n_gy, 2, q, kzw, q, 2, 2, cells))
    scale = 1.0 / (z.total_x * z.total_y * cells)
    for h in range(z.n_gy):
        ang = angle(h * kzw + np.arange(kzw), np.arange(cells), cells)
        c, s = np.cos(ang) * scale, np.sin(ang) * scale
        for i in range(q):
            for copy in range(2):
                zi[h, 0, i, :, i, 0, copy], zi[h, 1, i, :, i, 0, copy] = c, -s
                zi[h, 0, i, :, i, 1, copy], zi[h, 1, i, :, i, 1, copy] = s, c
    zi = two_terms(zi.reshape(z.n_gy, 1, LANES, q * 2 * LANES), 1)
    return zf, xf, xi, zi


def split(value):
    high = value.astype(jnp.bfloat16)
    return high, (value - high.astype(jnp.float32)).astype(jnp.bfloat16)


def dot(left, right):
    high, low = split(left)

    def one(a, b):
        return jnp.dot(a, b, preferred_element_type=jnp.float32)

    return one(high, right[0]) + (one(high, right[1]) + one(low, right[0]))


def times_i(value, sign):
    return pltpu.roll(value, LANES // 2, 1) * sign


def transform(values, direction, sign):
    count = len(values)
    if count == 1:
        return values
    even = transform(values[0::2], direction, sign)
    odd = transform(values[1::2], direction, sign)
    low, high = [], []
    for k in range(count // 2):
        value = odd[k]
        if k * 4 == count:
            value = times_i(value, sign * direction)
        elif k:
            theta = direction * 2.0 * math.pi * k / count
            value = value * math.cos(theta) + times_i(value, sign * math.sin(theta))
        low.append(even[k] + value)
        high.append(even[k] - value)
    return low + high


def exchange(values, lane, chunk):
    count = len(values)
    values = list(values)
    bit = 1
    while bit < count:
        keep = (lane // (chunk * bit)) % 2 == 0
        for i in range(count):
            if i & bit == 0:
                a, b = values[i], values[i | bit]
                values[i] = jnp.where(keep, a, pltpu.roll(b, chunk * bit, 1))
                values[i | bit] = jnp.where(keep, pltpu.roll(a, LANES - chunk * bit, 1), b)
        bit *= 2
    return values


def lane_tiles(value):
    return [value[:, i : i + LANES] for i in range(0, value.shape[1], LANES)]


def powers(value, highest):
    result = [None, value]
    for _ in range(highest - 1):
        result.append(result[-1] * value)
    return result


def scaled_mul(value, power):
    return value if power is None else value * power


def kernel_body(
    z, off_hbm, mass_hbm, gain_hbm, zf_hbm, xf_hbm, xi_hbm, zi_hbm, out_ref,
    off_ref, mass_ref, gain, zf, xf, xi, zi, yb, edge, xh, xc, near_src, acc_ref, mom, msg_b, got_b, spec, coef,
    msg_c, got_c, lines, field,
    load_sem, ysend, yrecv, hsend, hrecv, csend, crecv, bsend, brecv, fsend, frecv,
):
    nx, ny = z.n_gx, z.n_gy
    mx, my = lax.axis_index("gx"), lax.axis_index("gy")
    me = mx * ny + my
    total = nx * ny

    def wrap(index, count):
        return jnp.where(index >= count, index - count, index)

    def each_peer(act):
        for j in range(ny):
            py = wrap(my + j, ny)

            def body(k, carry):
                act(wrap(mx + k, nx), py)
                return carry

            lax.fori_loop(0 if j else 1, nx, body, 0)

    def all_of(buffer, count, sem):
        span = buffer.at[pl.ds(0, count)]
        pltpu.make_async_copy(span, span, sem).wait()

    barrier = pltpu.get_barrier_semaphore()

    def greet(px, py):
        pl.semaphore_signal(barrier, inc=1, device_id=(px, py), device_id_type=MESH)

    loads = [
        pltpu.make_async_copy(src, dst, load_sem.at[i])
        for i, (src, dst) in enumerate(
            [(off_hbm, off_ref), (mass_hbm, mass_ref), (zf_hbm.at[my], zf), (xf_hbm, xf), (xi_hbm, xi),
             (zi_hbm, zi), (gain_hbm, gain)]
        )
    ]
    for load in loads:
        load.start()
    each_peer(greet)
    loads[0].wait()
    loads[1].wait()

    for comp in range(4):
        value = off_ref[comp] if comp < 3 else mass_ref[...]
        yb[my, comp] = value
        edge[0, comp] = value[0:1]
        edge[1, comp] = value[z.rows_y - 1 : z.rows_y]

    pl.semaphore_wait(barrier, total - 1)

    y_copies = []
    for k in range(1, ny):
        to = lax.rem(my + k, ny)
        copy = pltpu.make_async_remote_copy(
            src_ref=yb.at[my], dst_ref=yb.at[my], send_sem=ysend.at[k], recv_sem=yrecv.at[my],
            device_id=(mx, to), device_id_type=MESH,
        )
        copy.start()
        y_copies.append(copy)
    h_copies = []
    for side in range(2):
        to_x = lax.rem(mx + (1 if side == 0 else nx - 1), nx)
        copy = pltpu.make_async_remote_copy(
            src_ref=yb.at[my], dst_ref=xh.at[side], send_sem=hsend.at[side], recv_sem=hrecv.at[side],
            device_id=(to_x, my), device_id_type=MESH,
        )
        copy.start()
        h_copies.append(copy)
        for end in range(2):
            to_y = lax.rem(my + (1 if end == 0 else ny - 1), ny)
            copy = pltpu.make_async_remote_copy(
                src_ref=edge.at[1 - end], dst_ref=xc.at[side, end], send_sem=csend.at[side, end],
                recv_sem=crecv.at[side, end], device_id=(to_x, to_y), device_id_type=MESH,
            )
            copy.start()
            h_copies.append(copy)

    lane = lax.broadcasted_iota(jnp.int32, (1, LANES), 1)
    first = lane < LANES // 2
    sign = jnp.where(first, -1.0, 1.0).astype(jnp.float32)
    rows, rows_pad = z.rows, z.rows_pad

    if rows_pad != rows:
        mom[...] = jnp.zeros_like(mom)

    def moments_of(block, slot):
        bodies = [yb[block, comp] for comp in range(4)]
        s, t, w = [2.0 * v - 1.0 for v in bodies[:3]]
        along_x, along_y = powers(s, 5), powers(t, 5)
        made = {}
        weighted = bodies[3]
        for e in range(2):
            if e:
                weighted = weighted * w
            for a in range(6 - e):
                partial = scaled_mul(weighted, along_x[a] if a else None)
                for b in range(6 - e - a):
                    tiles = lane_tiles(scaled_mul(partial, along_y[b] if b else None))
                    made[(a, b, e)] = functools.reduce(lambda x, y: x + y, tiles)
        for u in range(z.q // 2):
            for r in range(rows):
                pair = []
                for b in range(2):
                    c = (2 * u + b) * rows + r
                    pair.append(made[CHANNELS[c]] if c < COUNT else jnp.zeros_like(s[:, :LANES]))
                mixed = jnp.where(first, pair[0], pair[1])
                crossed = jnp.where(first, pair[1], pair[0])
                mixed = mixed + pltpu.roll(crossed, LANES // 2, 1)
                mom[u, slot, pl.ds(r, z.rows_y, stride=rows_pad), :] = mixed

    moments_of(my, my)
    for k in range(1, ny):
        source = lax.rem(my + k, ny)
        pltpu.make_async_remote_copy(
            src_ref=yb.at[source], dst_ref=yb.at[source], send_sem=ysend.at[k], recv_sem=yrecv.at[source],
            device_id=(mx, source), device_id_type=MESH,
        ).wait_recv()
        moments_of(source, source)
    loads[2].wait()
    height = ny * z.rows_y * rows_pad
    along = dot(mom[0].reshape(height, LANES), zf.at[0])
    for u in range(1, z.q // 2):
        along = along + dot(mom[u].reshape(height, LANES), zf.at[u])
    along = [along[i * rows_pad : (i + 1) * rows_pad] for i in range(z.total_y)]
    for ky, value in enumerate(transform(along, -1.0, sign)):
        msg_b[ky] = value[:rows]

    stride = 5 if nx % 5 else 1

    def send_b(k, carry):
        to = lax.rem(mx + stride * k, nx)
        pltpu.make_async_remote_copy(
            src_ref=msg_b.at[to], dst_ref=got_b.at[mx], send_sem=bsend, recv_sem=brecv,
            device_id=(to, my), device_id_type=MESH,
        ).start()
        return carry

    lax.fori_loop(1, nx, send_b, 0)
    got_b[mx] = msg_b[mx]

    ahead, behind = lax.rem(my + 1, ny), lax.rem(my + ny - 1, ny)

    def fill(dx, main, top, bottom):
        for comp in range(4):
            value = main(comp)
            below = jnp.concatenate([top(comp), value[: z.rows_y - 1]], axis=0)
            above = jnp.concatenate([value[1:], bottom(comp)], axis=0)
            for dy, moved in enumerate((below, value, above)):
                if comp == 0 and dx != 1:
                    moved = moved + (dx - 1.0)
                if comp == 1 and dy != 1:
                    moved = moved + (dy - 1.0)
                for j, tile in enumerate(lane_tiles(moved)):
                    near_src[(dx * 3 + dy) * (z.width // LANES) + j, comp] = tile

    tiles = z.width // LANES

    def near_steps(begin, end):
        target = [[off_ref[comp, :, j * LANES : (j + 1) * LANES] for j in range(tiles)] for comp in range(3)]
        init = tuple(acc_ref[comp, :, j * LANES : (j + 1) * LANES] for comp in range(3) for j in range(tiles))

        def step(index, carry):
            sums = [list(carry[comp * tiles : (comp + 1) * tiles]) for comp in range(3)]
            loaded = [near_src[index, comp] for comp in range(4)]
            turned = [pltpu.roll(v, LANES // 2, 1) for v in loaded]
            for half in range(2):
                both = [
                    jnp.where(first, a, b) if half == 0 else jnp.where(first, b, a)
                    for a, b in zip(loaded, turned)
                ]
                for dz in (-1, 0, 1):
                    src = both if dz == 0 else [pltpu.roll(v, (LANES - dz) % LANES, 1) for v in both]
                    src_z = src[2] + float(dz) if dz else src[2]
                    for j in range(tiles):
                        sx = src[0] - target[0][j]
                        sy = src[1] - target[1][j]
                        sz = src_z - target[2][j]
                        inv = lax.rsqrt(sx * sx + sy * sy + (sz * sz + SOFTEN * SOFTEN))
                        pull = (src[3] * inv) * (inv * inv)
                        sums[0][j] = sums[0][j] + sx * pull
                        sums[1][j] = sums[1][j] + sy * pull
                        sums[2][j] = sums[2][j] + sz * pull
            return tuple(v for comp in sums for v in comp)

        final = lax.fori_loop(begin, end, step, init)
        for comp in range(3):
            for j in range(tiles):
                acc_ref[comp, :, j * LANES : (j + 1) * LANES] = final[comp * tiles + j]

    acc_ref[...] = jnp.zeros_like(acc_ref)
    fill(
        1,
        lambda comp: off_ref[comp] if comp < 3 else mass_ref[...],
        lambda comp: yb[behind, comp, z.rows_y - 1 : z.rows_y],
        lambda comp: yb[ahead, comp, 0:1],
    )
    near_steps(3 * tiles, 6 * tiles)
    for copy in h_copies:
        copy.wait_recv()
    for side in range(2):
        fill(2 * side, lambda comp: xh[side, comp], lambda comp: xc[side, 0, comp], lambda comp: xc[side, 1, comp])
    near_steps(0, 3 * tiles)

    all_of(got_b, nx - 1, brecv)
    groups, q = z.groups, z.q
    deep = 2 * groups
    turned = exchange([got_b[i] for i in range(nx)], lane, z.wg)
    loads[3].wait()
    stacked = jnp.concatenate(
        [
            jnp.concatenate([turned[(0 * q + i) * groups + g], turned[(1 * q + i) * groups + g]], axis=1)
            for g in range(groups)
            for i in range(q)
        ],
        axis=0,
    )
    spectrum = dot(stacked, xf)
    for g in range(groups):
        part = spectrum[g * q * rows : g * q * rows + COUNT]
        part_re, part_im = part[:, :LANES], part[:, LANES:]
        for which, (front, back) in enumerate(((part_re, -part_im), (part_im, part_re))):
            spec[which, pl.ds(2 * g, COUNT, stride=deep), :] = front
            spec[which, pl.ds(2 * g + 1, COUNT, stride=deep), :] = back
    loads[6].wait()

    def couple(step, carry):
        members = [step * PER_STEP + i for i in range(PER_STEP)]
        sums = [[None, None] for _ in range(2 * PER_STEP)]
        for c in range(0, COUNT, 2):
            spec_two = [[spec[w, (c + i) * deep : (c + i + 1) * deep] for w in range(2)] for i in range(2)]
            for n in range(2 * PER_STEP):
                d = members[n // 2] + (n % 2) * HALF
                two = gain[d, c * deep : (c + 2) * deep, :].astype(jnp.float32)
                for i in range(2):
                    one = two[i * deep : (i + 1) * deep]
                    for w in range(2):
                        term = one * spec_two[i][w]
                        sums[n][w] = term if sums[n][w] is None else sums[n][w] + term
        for i, p in enumerate(members):
            own, other = sums[2 * i], sums[2 * i + 1]
            start = pl.multiple_of(p * deep, deep)
            coef[0, pl.ds(start, deep), :] = own[0] - other[1]
            coef[1, pl.ds(start, deep), :] = own[1] + other[0]
        return carry

    lax.fori_loop(0, HALF // PER_STEP, couple, 0)
    prow = z.prow
    height = q * prow
    pairs = []
    for g in range(groups):
        pair = jnp.concatenate(
            [
                coef[w, pl.ds(2 * g, HALF, stride=deep), :] + coef[w, pl.ds(2 * g + 1, HALF, stride=deep), :]
                for w in range(2)
            ],
            axis=1,
        )
        if height > HALF:
            pair = jnp.concatenate([pair, jnp.zeros((height - HALF, 2 * LANES), jnp.float32)], axis=0)
        pairs.append(pair)
    loads[4].wait()
    back = dot(jnp.concatenate(pairs, axis=0), xi)
    ordered = [
        back[g * height + i * prow : g * height + (i + 1) * prow, ri * LANES : (ri + 1) * LANES]
        for ri in range(2)
        for i in range(q)
        for g in range(groups)
    ]
    for x, value in enumerate(exchange(ordered, lane, z.wg)):
        msg_c[x] = value

    def send_c(px, py):
        pltpu.make_async_remote_copy(
            src_ref=msg_c.at[px], dst_ref=got_c.at[me], send_sem=fsend, recv_sem=frecv,
            device_id=(px, py), device_id_type=MESH,
        ).start()

    each_peer(send_c)
    got_c[me] = msg_c[mx]

    near_steps(6 * tiles, 9 * tiles)

    all_of(got_c, total - 1, frecv)
    loads[5].wait()
    prow_pad = z.prow_pad
    if prow_pad != prow:
        lines[:, :, prow:, :] = jnp.zeros(lines.shape[:2] + (prow_pad - prow, LANES), jnp.float32)
    result = None
    for h in range(ny):
        for y, value in enumerate(transform([got_c[k * ny + h] for k in range(nx)], 1.0, sign)):
            lines[h, y, :prow] = value
        own = lines[h, pl.ds(my * z.rows_y, z.rows_y)].reshape(z.rows_y * prow_pad, LANES)
        term = dot(own, zi.at[h])
        result = term if result is None else result + term
    for column, tile in enumerate(lane_tiles(result)):
        field[column] = tile

    def coefficient(c):
        part, p = c // HALF, c % HALF
        i, r = p // prow, p % prow
        return field[i * 2 + part, pl.ds(r, z.rows_y, stride=prow_pad), :]

    number = {channel: c for c, channel in enumerate(CHANNELS)}
    for j in range(tiles):
        lanes = slice(j * LANES, (j + 1) * LANES)
        s, t, w = [2.0 * off_ref[comp, :, lanes] - 1.0 for comp in range(3)]
        along = []
        for e in range(2):
            value = slope_x = slope_y = None
            for b in reversed(range(6 - e)):
                top = 5 - e - b
                inner = coefficient(number[(top, b, e)])
                slope = None
                for a in reversed(range(top)):
                    slope = inner if slope is None else slope * s + inner
                    inner = inner * s + coefficient(number[(a, b, e)])
                slope_y = value if slope_y is None else slope_y * t + value
                value = inner if value is None else value * t + inner
                if slope is not None:
                    slope_x = slope if slope_x is None else slope_x * t + slope
            along.append((value, slope_x, slope_y))
        out_ref[0, :, lanes] = acc_ref[0, :, lanes] - (along[0][1] + w * along[1][1])
        out_ref[1, :, lanes] = acc_ref[1, :, lanes] - (along[0][2] + w * along[1][2])
        out_ref[2, :, lanes] = acc_ref[2, :, lanes] - along[1][0]

    for copy in y_copies:
        copy.wait_send()
    for copy in h_copies:
        copy.wait_send()

    all_of(got_b, nx - 1, bsend)
    all_of(got_c, total - 1, fsend)


def local(offsets, masses, kernel):
    n_gx, n_gy = lax.axis_size("gx"), lax.axis_size("gy")
    _, planes_x, rows_y, width = offsets.shape
    waves = kernel.shape[3] * kernel.shape[4]
    z = Sizes(n_gx, n_gy, planes_x, rows_y, width, waves)
    made = tables(z)
    f32, bf16 = jnp.float32, jnp.bfloat16
    tiles = width // LANES
    scratch = [
        pltpu.VMEM((3, rows_y, width), f32),
        pltpu.VMEM((rows_y, width), f32),
        pltpu.VMEM((COUNT, COUNT * 2 * z.groups, LANES), kernel.dtype),
        pltpu.VMEM(made[0].shape[1:], bf16),
        pltpu.VMEM(made[1].shape, bf16),
        pltpu.VMEM(made[2].shape, bf16),
        pltpu.VMEM(made[3].shape, bf16),
        pltpu.VMEM((n_gy, 4, rows_y, width), f32),
        pltpu.VMEM((2, 4, 1, width), f32),
        pltpu.VMEM((2, 4, rows_y, width), f32),
        pltpu.VMEM((2, 2, 4, 1, width), f32),
        pltpu.VMEM((9 * tiles, 4, rows_y, LANES), f32),
        pltpu.VMEM((3, rows_y, width), f32),
        pltpu.VMEM((z.q // 2, n_gy, rows_y * z.rows_pad, LANES), f32),
        pltpu.VMEM((n_gx, z.rows, LANES), f32),
        pltpu.VMEM((n_gx, z.rows, LANES), f32),
        pltpu.VMEM((2, COUNT * 2 * z.groups, LANES), f32),
        pltpu.VMEM((2, HALF * 2 * z.groups, LANES), f32),
        pltpu.VMEM((n_gx, z.prow, LANES), f32),
        pltpu.VMEM((n_gy * n_gx, z.prow, LANES), f32),
        pltpu.VMEM((n_gy, n_gx, z.prow_pad, LANES), f32),
        pltpu.VMEM((z.q * 2, rows_y * z.prow_pad, LANES), f32),
        pltpu.SemaphoreType.DMA((7,)),
        pltpu.SemaphoreType.DMA((n_gy,)),
        pltpu.SemaphoreType.DMA((n_gy,)),
        pltpu.SemaphoreType.DMA((2,)),
        pltpu.SemaphoreType.DMA((2,)),
        pltpu.SemaphoreType.DMA((2, 2)),
        pltpu.SemaphoreType.DMA((2, 2)),
        pltpu.SemaphoreType.DMA,
        pltpu.SemaphoreType.DMA,
        pltpu.SemaphoreType.DMA,
        pltpu.SemaphoreType.DMA,
    ]
    gains = jnp.transpose(kernel.reshape(COUNT, 2, COUNT, z.groups, LANES), (0, 2, 3, 1, 4))
    gains = gains.reshape(COUNT, COUNT * 2 * z.groups, LANES)
    out = pl.pallas_call(
        functools.partial(kernel_body, z),
        out_shape=jax.ShapeDtypeStruct((3, rows_y, width), f32),
        in_specs=[pl.BlockSpec(memory_space=pltpu.HBM)] * 7,
        out_specs=pl.BlockSpec(memory_space=pltpu.VMEM),
        scratch_shapes=scratch,
        compiler_params=pltpu.CompilerParams(
            collective_id=0, has_side_effects=True, vmem_limit_bytes=62 * 1024 * 1024
        ),
    )(
        offsets.reshape(3, rows_y, width), masses.reshape(rows_y, width),
        gains, *[jnp.asarray(t) for t in made],
    )
    return out.reshape(3, planes_x, rows_y, width)


def solution(mesh):
    placed = (P(None, "gx", "gy", None), P("gx", "gy", None), P(None, None, None, "gx", "gy"))
    return jax.shard_map(
        local, mesh=mesh, in_specs=placed, out_specs=P(None, "gx", "gy", None), check_vma=False
    )
```

```python
import functools
import math

import jax
import jax.numpy as jnp
import numpy as np
from jax import lax
from jax.experimental import pallas as pl
from jax.experimental.pallas import tpu as pltpu
from jax.sharding import PartitionSpec as P

BODIES = 8
SOFTEN = 0.5
LANES = 128
PER_STEP = 2
MESH = pl.DeviceIdType.MESH


def channel_list():
    listed = []
    for pow_z in range(2):
        for pow_x in range(6 - pow_z):
            for pow_y in range(6 - pow_z - pow_x):
                listed.append((pow_x, pow_y, pow_z))
    return listed


CHANNELS = channel_list()
COUNT = len(CHANNELS)
HALF = COUNT // 2


class Sizes:
    def __init__(self, n_gx, n_gy, planes_x, rows_y, row_width, waves):
        self.n_gx, self.n_gy = n_gx, n_gy
        self.rows_y = rows_y
        self.cells_z = row_width // BODIES
        self.width = row_width
        self.total_x = planes_x * n_gx
        self.total_y = rows_y * n_gy
        self.kzw = self.cells_z // n_gy
        self.q = LANES // (2 * self.kzw)
        self.groups = waves // LANES
        self.wg = LANES // self.total_x
        self.rows = -(-COUNT // self.q)
        self.rows_pad = -(-self.rows // 8) * 8
        self.prow = -(-HALF // self.q)
        self.prow_pad = -(-self.prow // 8) * 8
        assert planes_x == 1 and self.total_y == n_gx and rows_y == 8
        assert 2 * self.cells_z == LANES and self.q % 2 == 0
        assert 2 * self.q * self.groups == self.total_x and self.groups == 4


def angle(left, right, length):
    return (np.multiply.outer(left, right) % length) * (2.0 * math.pi / length)


def two_terms(table, dim):
    table = np.asarray(table, np.float32)
    high = table.astype(jnp.bfloat16)
    low = (table - high.astype(np.float32)).astype(jnp.bfloat16)
    return np.concatenate([high, low], axis=dim)


def tables(z):
    cells, kzw, q, wg, nx = z.cells_z, z.kzw, z.q, z.wg, z.total_x
    zf = np.zeros((z.n_gy, q // 2, 2, cells, 2, q, kzw))
    for h in range(z.n_gy):
        ang = angle(np.arange(cells), h * kzw + np.arange(kzw), cells)
        for u in range(q // 2):
            for b in range(2):
                zf[h, u, b, :, 0, 2 * u + b] = np.cos(ang)
                zf[h, u, b, :, 1, 2 * u + b] = -np.sin(ang)
    zf = two_terms(zf.reshape(z.n_gy, q // 2, 1, LANES, LANES), 2)
    ang = angle(np.arange(nx), np.arange(nx), nx)
    c, s = np.cos(ang), np.sin(ang)
    xf = np.zeros((2, nx, wg, 2, wg, nx))
    xi = np.zeros((2, wg, nx, 2, nx, wg))
    for k in range(wg):
        xf[0, :, k, 0, k], xf[1, :, k, 0, k] = c, s
        xf[0, :, k, 1, k], xf[1, :, k, 1, k] = -s, c
        xi[0, k, :, 0, :, k], xi[1, k, :, 0, :, k] = c, -s
        xi[0, k, :, 1, :, k], xi[1, k, :, 1, :, k] = s, c
    xf = two_terms(xf.reshape(1, 2 * LANES, 2 * LANES), 0)
    xi = two_terms(xi.reshape(1, 2 * LANES, 2 * LANES), 0)
    zi = np.zeros((z.n_gy, 2, q, kzw, q, 2, 2, cells))
    scale = 1.0 / (z.total_x * z.total_y * cells)
    for h in range(z.n_gy):
        ang = angle(h * kzw + np.arange(kzw), np.arange(cells), cells)
        c, s = np.cos(ang) * scale, np.sin(ang) * scale
        for i in range(q):
            for copy in range(2):
                zi[h, 0, i, :, i, 0, copy], zi[h, 1, i, :, i, 0, copy] = c, -s
                zi[h, 0, i, :, i, 1, copy], zi[h, 1, i, :, i, 1, copy] = s, c
    zi = two_terms(zi.reshape(z.n_gy, 1, LANES, q * 2 * LANES), 1)
    return zf, xf, xi, zi


def split(value):
    high = value.astype(jnp.bfloat16)
    return high, (value - high.astype(jnp.float32)).astype(jnp.bfloat16)


def dot(left, right):
    high, low = split(left)

    def one(a, b):
        return jnp.dot(a, b, preferred_element_type=jnp.float32)

    return one(high, right[0]) + (one(high, right[1]) + one(low, right[0]))


def times_i(value, sign):
    return pltpu.roll(value, LANES // 2, 1) * sign


def transform(values, direction, sign):
    count = len(values)
    if count == 1:
        return values
    even = transform(values[0::2], direction, sign)
    odd = transform(values[1::2], direction, sign)
    low, high = [], []
    for k in range(count // 2):
        value = odd[k]
        if k * 4 == count:
            value = times_i(value, sign * direction)
        elif k:
            theta = direction * 2.0 * math.pi * k / count
            value = value * math.cos(theta) + times_i(value, sign * math.sin(theta))
        low.append(even[k] + value)
        high.append(even[k] - value)
    return low + high


def exchange(values, lane, chunk):
    count = len(values)
    values = list(values)
    bit = 1
    while bit < count:
        keep = (lane // (chunk * bit)) % 2 == 0
        for i in range(count):
            if i & bit == 0:
                a, b = values[i], values[i | bit]
                values[i] = jnp.where(keep, a, pltpu.roll(b, chunk * bit, 1))
                values[i | bit] = jnp.where(keep, pltpu.roll(a, LANES - chunk * bit, 1), b)
        bit *= 2
    return values


def lane_tiles(value):
    return [value[:, i : i + LANES] for i in range(0, value.shape[1], LANES)]


def powers(value, highest):
    result = [None, value]
    for _ in range(highest - 1):
        result.append(result[-1] * value)
    return result


def scaled_mul(value, power):
    return value if power is None else value * power


def kernel_body(
    z, off_hbm, mass_hbm, gain_hbm, zf_hbm, xf_hbm, xi_hbm, zi_hbm, out_ref,
    off_ref, mass_ref, gain, zf, xf, xi, zi, yb, edge, xh, xc, near_src, acc_ref, mom, msg_b, got_b, spec, coef,
    msg_c, got_c, lines, field,
    load_sem, ysend, yrecv, hsend, hrecv, csend, crecv, bsend, brecv, fsend, frecv,
):
    nx, ny = z.n_gx, z.n_gy
    mx, my = lax.axis_index("gx"), lax.axis_index("gy")
    me = mx * ny + my
    total = nx * ny

    def wrap(index, count):
        return jnp.where(index >= count, index - count, index)

    def each_peer(act):
        for j in range(ny):
            py = wrap(my + j, ny)

            def body(k, carry):
                act(wrap(mx + k, nx), py)
                return carry

            lax.fori_loop(0 if j else 1, nx, body, 0)

    def all_of(buffer, count, sem):
        span = buffer.at[pl.ds(0, count)]
        pltpu.make_async_copy(span, span, sem).wait()

    barrier = pltpu.get_barrier_semaphore()

    def greet(px, py):
        pl.semaphore_signal(barrier, inc=1, device_id=(px, py), device_id_type=MESH)

    loads = [
        pltpu.make_async_copy(src, dst, load_sem.at[i])
        for i, (src, dst) in enumerate(
            [(off_hbm, off_ref), (mass_hbm, mass_ref), (zf_hbm.at[my], zf), (xf_hbm, xf), (xi_hbm, xi),
             (zi_hbm, zi), (gain_hbm, gain)]
        )
    ]
    for load in loads:
        load.start()
    each_peer(greet)
    loads[0].wait()
    loads[1].wait()

    for comp in range(4):
        value = off_ref[comp] if comp < 3 else mass_ref[...]
        yb[my, comp] = value
        edge[0, comp] = value[0:1]
        edge[1, comp] = value[z.rows_y - 1 : z.rows_y]

    pl.semaphore_wait(barrier, total - 1)

    y_copies = []
    for k in range(1, ny):
        to = lax.rem(my + k, ny)
        copy = pltpu.make_async_remote_copy(
            src_ref=yb.at[my], dst_ref=yb.at[my], send_sem=ysend.at[k], recv_sem=yrecv.at[my],
            device_id=(mx, to), device_id_type=MESH,
        )
        copy.start()
        y_copies.append(copy)
    h_copies = []
    for side in range(2):
        to_x = lax.rem(mx + (1 if side == 0 else nx - 1), nx)
        copy = pltpu.make_async_remote_copy(
            src_ref=yb.at[my], dst_ref=xh.at[side], send_sem=hsend.at[side], recv_sem=hrecv.at[side],
            device_id=(to_x, my), device_id_type=MESH,
        )
        copy.start()
        h_copies.append(copy)
        for end in range(2):
            to_y = lax.rem(my + (1 if end == 0 else ny - 1), ny)
            copy = pltpu.make_async_remote_copy(
                src_ref=edge.at[1 - end], dst_ref=xc.at[side, end], send_sem=csend.at[side, end],
                recv_sem=crecv.at[side, end], device_id=(to_x, to_y), device_id_type=MESH,
            )
            copy.start()
            h_copies.append(copy)

    lane = lax.broadcasted_iota(jnp.int32, (1, LANES), 1)
    first = lane < LANES // 2
    sign = jnp.where(first, -1.0, 1.0).astype(jnp.float32)
    rows, rows_pad = z.rows, z.rows_pad

    if rows_pad != rows:
        mom[...] = jnp.zeros_like(mom)

    def moments_of(block, slot):
        bodies = [yb[block, comp] for comp in range(4)]
        s, t, w = [2.0 * v - 1.0 for v in bodies[:3]]
        along_x, along_y = powers(s, 5), powers(t, 5)
        made = {}
        weighted = bodies[3]
        for e in range(2):
            if e:
                weighted = weighted * w
            for a in range(6 - e):
                partial = scaled_mul(weighted, along_x[a] if a else None)
                for b in range(6 - e - a):
                    tiles = lane_tiles(scaled_mul(partial, along_y[b] if b else None))
                    made[(a, b, e)] = functools.reduce(lambda x, y: x + y, tiles)
        for u in range(z.q // 2):
            for r in range(rows):
                pair = []
                for b in range(2):
                    c = (2 * u + b) * rows + r
                    pair.append(made[CHANNELS[c]] if c < COUNT else jnp.zeros_like(s[:, :LANES]))
                mixed = jnp.where(first, pair[0], pair[1])
                crossed = jnp.where(first, pair[1], pair[0])
                mixed = mixed + pltpu.roll(crossed, LANES // 2, 1)
                mom[u, slot, pl.ds(r, z.rows_y, stride=rows_pad), :] = mixed

    moments_of(my, my)
    for k in range(1, ny):
        source = lax.rem(my + k, ny)
        pltpu.make_async_remote_copy(
            src_ref=yb.at[source], dst_ref=yb.at[source], send_sem=ysend.at[k], recv_sem=yrecv.at[source],
            device_id=(mx, source), device_id_type=MESH,
        ).wait_recv()
        moments_of(source, source)
    loads[2].wait()
    height = ny * z.rows_y * rows_pad
    along = dot(mom[0, :ny].reshape(height, LANES), zf.at[0])
    for u in range(1, z.q // 2):
        along = along + dot(mom[u, :ny].reshape(height, LANES), zf.at[u])
    along = [along[i * rows_pad : (i + 1) * rows_pad] for i in range(z.total_y)]
    for ky, value in enumerate(transform(along, -1.0, sign)):
        msg_b[ky] = value[:rows]

    stride = 5 if nx % 5 else 1

    def send_b(k, carry):
        to = lax.rem(mx + stride * k, nx)
        pltpu.make_async_remote_copy(
            src_ref=msg_b.at[to], dst_ref=got_b.at[mx], send_sem=bsend, recv_sem=brecv,
            device_id=(to, my), device_id_type=MESH,
        ).start()
        return carry

    lax.fori_loop(1, nx, send_b, 0)
    got_b[mx] = msg_b[mx]

    ahead, behind = lax.rem(my + 1, ny), lax.rem(my + ny - 1, ny)

    def fill(dx, main, top, bottom):
        for comp in range(4):
            value = main(comp)
            below = jnp.concatenate([top(comp), value[: z.rows_y - 1]], axis=0)
            above = jnp.concatenate([value[1:], bottom(comp)], axis=0)
            for dy, moved in enumerate((below, value, above)):
                if comp == 0 and dx != 1:
                    moved = moved + (dx - 1.0)
                if comp == 1 and dy != 1:
                    moved = moved + (dy - 1.0)
                for j, tile in enumerate(lane_tiles(moved)):
                    near_src[(dx * 3 + dy) * (z.width // LANES) + j, comp] = tile

    tiles = z.width // LANES

    def near_steps(begin, end):
        target = [[off_ref[comp, :, j * LANES : (j + 1) * LANES] for j in range(tiles)] for comp in range(3)]
        init = tuple(acc_ref[comp, :, j * LANES : (j + 1) * LANES] for comp in range(3) for j in range(tiles))

        def step(index, carry):
            sums = [list(carry[comp * tiles : (comp + 1) * tiles]) for comp in range(3)]
            loaded = [near_src[index, comp] for comp in range(4)]
            turned = [pltpu.roll(v, LANES // 2, 1) for v in loaded]
            for half in range(2):
                both = [
                    jnp.where(first, a, b) if half == 0 else jnp.where(first, b, a)
                    for a, b in zip(loaded, turned)
                ]
                for dz in (-1, 0, 1):
                    src = both if dz == 0 else [pltpu.roll(v, (LANES - dz) % LANES, 1) for v in both]
                    src_z = src[2] + float(dz) if dz else src[2]
                    for j in range(tiles):
                        sx = src[0] - target[0][j]
                        sy = src[1] - target[1][j]
                        sz = src_z - target[2][j]
                        inv = lax.rsqrt(sx * sx + sy * sy + (sz * sz + SOFTEN * SOFTEN))
                        pull = (src[3] * inv) * (inv * inv)
                        sums[0][j] = sums[0][j] + sx * pull
                        sums[1][j] = sums[1][j] + sy * pull
                        sums[2][j] = sums[2][j] + sz * pull
            return tuple(v for comp in sums for v in comp)

        final = lax.fori_loop(begin, end, step, init)
        for comp in range(3):
            for j in range(tiles):
                acc_ref[comp, :, j * LANES : (j + 1) * LANES] = final[comp * tiles + j]

    acc_ref[...] = jnp.zeros_like(acc_ref)
    fill(
        1,
        lambda comp: off_ref[comp] if comp < 3 else mass_ref[...],
        lambda comp: yb[behind, comp, z.rows_y - 1 : z.rows_y],
        lambda comp: yb[ahead, comp, 0:1],
    )
    near_steps(3 * tiles, 6 * tiles)
    for copy in h_copies:
        copy.wait_recv()
    for side in range(2):
        fill(2 * side, lambda comp: xh[side, comp], lambda comp: xc[side, 0, comp], lambda comp: xc[side, 1, comp])
    near_steps(0, 3 * tiles)

    all_of(got_b, nx - 1, brecv)
    groups, q = z.groups, z.q
    deep = 2 * groups
    turned = exchange([got_b[i] for i in range(nx)], lane, z.wg)
    loads[3].wait()
    stacked = jnp.concatenate(
        [
            jnp.concatenate([turned[(0 * q + i) * groups + g], turned[(1 * q + i) * groups + g]], axis=1)
            for g in range(groups)
            for i in range(q)
        ],
        axis=0,
    )
    spectrum = dot(stacked, xf)
    for g in range(groups):
        part = spectrum[g * q * rows : g * q * rows + COUNT]
        part_re, part_im = part[:, :LANES], part[:, LANES:]
        for which, (front, back) in enumerate(((part_re, -part_im), (part_im, part_re))):
            spec[which, pl.ds(2 * g, COUNT, stride=deep), :] = front
            spec[which, pl.ds(2 * g + 1, COUNT, stride=deep), :] = back
    loads[6].wait()

    def couple(step, carry):
        members = [step * PER_STEP + i for i in range(PER_STEP)]
        sums = [[None, None] for _ in range(2 * PER_STEP)]
        for c in range(0, COUNT, 2):
            spec_two = [[spec[w, (c + i) * deep : (c + i + 1) * deep] for w in range(2)] for i in range(2)]
            for n in range(2 * PER_STEP):
                d = members[n // 2] + (n % 2) * HALF
                two = gain[d, c * deep : (c + 2) * deep, :].astype(jnp.float32)
                for i in range(2):
                    one = two[i * deep : (i + 1) * deep]
                    for w in range(2):
                        term = one * spec_two[i][w]
                        sums[n][w] = term if sums[n][w] is None else sums[n][w] + term
        for i, p in enumerate(members):
            own, other = sums[2 * i], sums[2 * i + 1]
            start = pl.multiple_of(p * deep, deep)
            coef[0, pl.ds(start, deep), :] = own[0] - other[1]
            coef[1, pl.ds(start, deep), :] = own[1] + other[0]
        return carry

    lax.fori_loop(0, HALF // PER_STEP, couple, 0)
    prow = z.prow
    height = q * prow
    pairs = []
    for g in range(groups):
        pair = jnp.concatenate(
            [
                coef[w, pl.ds(2 * g, HALF, stride=deep), :] + coef[w, pl.ds(2 * g + 1, HALF, stride=deep), :]
                for w in range(2)
            ],
            axis=1,
        )
        if height > HALF:
            pair = jnp.concatenate([pair, jnp.zeros((height - HALF, 2 * LANES), jnp.float32)], axis=0)
        pairs.append(pair)
    loads[4].wait()
    back = dot(jnp.concatenate(pairs, axis=0), xi)
    ordered = [
        back[g * height + i * prow : g * height + (i + 1) * prow, ri * LANES : (ri + 1) * LANES]
        for ri in range(2)
        for i in range(q)
        for g in range(groups)
    ]
    for x, value in enumerate(exchange(ordered, lane, z.wg)):
        msg_c[x] = value

    def send_c(px, py):
        pltpu.make_async_remote_copy(
            src_ref=msg_c.at[px], dst_ref=got_c.at[me], send_sem=fsend, recv_sem=frecv,
            device_id=(px, py), device_id_type=MESH,
        ).start()

    each_peer(send_c)
    got_c[me] = msg_c[mx]

    near_steps(6 * tiles, 9 * tiles)

    all_of(got_c, total - 1, frecv)
    loads[5].wait()
    prow_pad = z.prow_pad
    if prow_pad != prow:
        lines[:, :, prow:, :] = jnp.zeros(lines.shape[:2] + (prow_pad - prow, LANES), jnp.float32)
    result = None
    for h in range(ny):
        for y, value in enumerate(transform([got_c[k * ny + h] for k in range(nx)], 1.0, sign)):
            lines[h, y, :prow] = value
        own = lines[h, pl.ds(my * z.rows_y, z.rows_y)].reshape(z.rows_y * prow_pad, LANES)
        term = dot(own, zi.at[h])
        result = term if result is None else result + term
    for column, tile in enumerate(lane_tiles(result)):
        field[column, : z.rows_y * prow_pad] = tile

    def coefficient(c):
        part, p = c // HALF, c % HALF
        i, r = p // prow, p % prow
        return field[i * 2 + part, pl.ds(r, z.rows_y, stride=prow_pad), :]

    number = {channel: c for c, channel in enumerate(CHANNELS)}
    for j in range(tiles):
        lanes = slice(j * LANES, (j + 1) * LANES)
        s, t, w = [2.0 * off_ref[comp, :, lanes] - 1.0 for comp in range(3)]
        along = []
        for e in range(2):
            value = slope_x = slope_y = None
            for b in reversed(range(6 - e)):
                top = 5 - e - b
                inner = coefficient(number[(top, b, e)])
                slope = None
                for a in reversed(range(top)):
                    slope = inner if slope is None else slope * s + inner
                    inner = inner * s + coefficient(number[(a, b, e)])
                slope_y = value if slope_y is None else slope_y * t + value
                value = inner if value is None else value * t + inner
                if slope is not None:
                    slope_x = slope if slope_x is None else slope_x * t + slope
            along.append((value, slope_x, slope_y))
        out_ref[0, :, lanes] = acc_ref[0, :, lanes] - (along[0][1] + w * along[1][1])
        out_ref[1, :, lanes] = acc_ref[1, :, lanes] - (along[0][2] + w * along[1][2])
        out_ref[2, :, lanes] = acc_ref[2, :, lanes] - along[1][0]

    for copy in y_copies:
        copy.wait_send()
    for copy in h_copies:
        copy.wait_send()

    all_of(got_b, nx - 1, bsend)
    all_of(got_c, total - 1, fsend)


def local(offsets, masses, kernel):
    n_gx, n_gy = lax.axis_size("gx"), lax.axis_size("gy")
    _, planes_x, rows_y, width = offsets.shape
    waves = kernel.shape[3] * kernel.shape[4]
    z = Sizes(n_gx, n_gy, planes_x, rows_y, width, waves)
    made = tables(z)
    f32, bf16 = jnp.float32, jnp.bfloat16
    tiles = width // LANES
    scratch = [
        pltpu.VMEM((3, rows_y, width), f32),
        pltpu.VMEM((rows_y, width), f32),
        pltpu.VMEM((COUNT, COUNT * 2 * z.groups, LANES), kernel.dtype),
        pltpu.VMEM(made[0].shape[1:], bf16),
        pltpu.VMEM(made[1].shape, bf16),
        pltpu.VMEM(made[2].shape, bf16),
        pltpu.VMEM(made[3].shape, bf16),
        pltpu.VMEM((n_gy, 4, rows_y, width), f32),
        pltpu.VMEM((2, 4, 1, width), f32),
        pltpu.VMEM((2, 4, rows_y, width), f32),
        pltpu.VMEM((2, 2, 4, 1, width), f32),
        pltpu.VMEM((9 * tiles, 4, rows_y, LANES), f32),
        pltpu.VMEM((3, rows_y, width), f32),
        pltpu.VMEM((z.q // 2, n_gy + 1, rows_y * z.rows_pad, LANES), f32),
        pltpu.VMEM((n_gx, z.rows, LANES), f32),
        pltpu.VMEM((n_gx, z.rows, LANES), f32),
        pltpu.VMEM((2, -(-COUNT // 8) * 16 * z.groups, LANES), f32),
        pltpu.VMEM((2, -(-HALF // 8) * 16 * z.groups, LANES), f32),
        pltpu.VMEM((n_gx, z.prow, LANES), f32),
        pltpu.VMEM((n_gy * n_gx, z.prow, LANES), f32),
        pltpu.VMEM((n_gy, n_gx, z.prow_pad, LANES), f32),
        pltpu.VMEM((z.q * 2, (rows_y + 1) * z.prow_pad, LANES), f32),
        pltpu.SemaphoreType.DMA((7,)),
        pltpu.SemaphoreType.DMA((n_gy,)),
        pltpu.SemaphoreType.DMA((n_gy,)),
        pltpu.SemaphoreType.DMA((2,)),
        pltpu.SemaphoreType.DMA((2,)),
        pltpu.SemaphoreType.DMA((2, 2)),
        pltpu.SemaphoreType.DMA((2, 2)),
        pltpu.SemaphoreType.DMA,
        pltpu.SemaphoreType.DMA,
        pltpu.SemaphoreType.DMA,
        pltpu.SemaphoreType.DMA,
    ]
    gains = jnp.transpose(kernel.reshape(COUNT, 2, COUNT, z.groups, LANES), (0, 2, 3, 1, 4))
    gains = gains.reshape(COUNT, COUNT * 2 * z.groups, LANES)
    out = pl.pallas_call(
        functools.partial(kernel_body, z),
        out_shape=jax.ShapeDtypeStruct((3, rows_y, width), f32),
        in_specs=[pl.BlockSpec(memory_space=pltpu.HBM)] * 7,
        out_specs=pl.BlockSpec(memory_space=pltpu.VMEM),
        scratch_shapes=scratch,
        compiler_params=pltpu.CompilerParams(
            collective_id=0, has_side_effects=True, vmem_limit_bytes=62 * 1024 * 1024
        ),
    )(
        offsets.reshape(3, rows_y, width), masses.reshape(rows_y, width),
        gains, *[jnp.asarray(t) for t in made],
    )
    return out.reshape(3, planes_x, rows_y, width)


def solution(mesh):
    placed = (P(None, "gx", "gy", None), P("gx", "gy", None), P(None, None, None, "gx", "gy"))
    return jax.shard_map(
        local, mesh=mesh, in_specs=placed, out_specs=P(None, "gx", "gy", None), check_vma=False
    )
```
